32 devices in a mesh: seq: 16 (over z, x, core), head: 2 (over y).
Axes of the slice: x: 2, y: 2, z: 4, core: 2. Of those that a mesh axis runs over, the one named last changes fastest.
Arguments:
- queries: bfloat16 [3072, 5120], P('seq', 'head'), may hold values from -8 to 8
- cur_keys: bfloat16 [3072, 5120], P('seq', 'head'), may hold values from -8 to 8
- cur_values: bfloat16 [3072, 5120], P('seq', 'head'), may hold values from -6 to 6
- hist_keys: bfloat16 [7168, 5120], P('seq', 'head'), may hold values from -8 to 8
- hist_values: bfloat16 [7168, 5120], P('seq', 'head'), may hold values from -6 to 6
- piece_readers: int32 [224, 2], P('seq'), may hold values from 0 to 15, as said below
- out_weight: bfloat16 [5120, 5120], P('head'), may hold values from -0.3125 to 0.3125
Outputs:
- attn_out: bfloat16 [3072, 5120], P('seq', 'head')
The draws below stay inside these ranges and needn't reach their ends.
Inputs may be any that keep to these rules, and one draw needn't show every extreme that they name: `piece_readers`: row j names 2 different reader blocks (indices of seq); piece j is held by index j // 14 of seq. One holder sends at most 2 pieces to one reader block: each holder sends to exactly 14 reader blocks, 2 pieces to each, and in every draw one reader block receives 2 pieces from every holder.
All inputs are finite; a program needn't handle non-finite values.
Results may differ from the reference program's by a relative error of at most 0.018.
Values may be sent and summed in bfloat16 or wider, within the bound.
A program may use at most 192 MiB of HBM per device.

```python
import math
import jax
import jax.numpy as jnp
from jax import lax

HEADS = 40
HDIM = 128
D = 5120
TOK_DEV = 192
TOKENS = 3072
PIECE = 32
HP_DEV = 14
TOP = 2
CAP = 2
READERS = 16
HPIECES = 224
HISTORY = 7168


def draw_queries(key, part):
    key = jax.random.fold_in(key, 11)
    own_rows = 1.6 * jax.random.normal(key, (TOKENS, D), jnp.float32)
    return jnp.clip(own_rows, -8.0, 8.0).astype(jnp.bfloat16)


def draw_cur_keys(key, part):
    key = jax.random.fold_in(key, 12)
    own_rows = 1.6 * jax.random.normal(key, (TOKENS, D), jnp.float32)
    return jnp.clip(own_rows, -8.0, 8.0).astype(jnp.bfloat16)


def draw_piece_readers(key, part):
    key = jax.random.fold_in(key, 21)
    hot_key, order_key, rank_key = jax.random.split(key, 3)
    hot_reader = jax.random.randint(hot_key, (), 0, READERS)
    reader_ids = jnp.arange(READERS, dtype=jnp.int32)
    order_noise = jax.random.randint(order_key, (READERS, READERS), 0, 1 << 20)
    order_score = order_noise * READERS + reader_ids[None, :]
    order_score = jnp.where(reader_ids[None, :] == hot_reader, -1, order_score)
    reader_order = jnp.argsort(order_score, axis=1).astype(jnp.int32)
    rank_noise = jax.random.randint(rank_key, (READERS, TOP, HP_DEV), 0, 1 << 20)
    rank_score = rank_noise * HP_DEV + jnp.arange(HP_DEV, dtype=jnp.int32)[None, None, :]
    piece_rank = jnp.argsort(rank_score, axis=2).astype(jnp.int32)
    top_ids = jnp.arange(TOP, dtype=jnp.int32)
    slot_ids = top_ids[None, :, None] * (HP_DEV // CAP) + piece_rank // CAP
    spread_order = jnp.broadcast_to(reader_order[:, None, :], (READERS, TOP, READERS))
    chosen = jnp.take_along_axis(spread_order, slot_ids, axis=2)
    return jnp.transpose(chosen, (0, 2, 1)).reshape(HPIECES, TOP).astype(jnp.int32)


def block_levels(own_key, extent, cuts, least, high):
    level = 1.0
    for position, shards_of in cuts:
        heights = jax.random.uniform(jax.random.fold_in(jax.random.fold_in(own_key, 6), position), (shards_of,), jnp.float32, least / len(cuts), high / len(cuts))
        level = level * jnp.repeat(jnp.exp(heights), extent[position] // shards_of).reshape((-1,) + (1,) * (len(extent) - 1 - position))
    return level


def gaussian(rng, extent, deviation, bound, pieces=(), held_as=jnp.bfloat16):
    gain = block_levels(rng, extent, pieces, -0.22, 0.18) if pieces else 1.0
    drawn = jax.random.normal(rng, extent, jnp.float32) * deviation * gain
    return jnp.minimum(jnp.maximum(drawn, -bound), bound).astype(held_as)


def setup_inputs(seed: int = 0) -> dict:
    splits = jax.random.split(jax.random.key(seed), 8)
    return {
        "queries": draw_queries(jax.random.fold_in(splits[7], 71), 0),
        "cur_keys": draw_cur_keys(jax.random.fold_in(splits[7], 71), 0),
        "cur_values": gaussian(splits[2], (TOKENS, D), 1.0, 6.0, ((0, 16), (1, 2))),
        "hist_keys": gaussian(splits[3], (HISTORY, D), 1.6, 8.0, ((0, 16), (1, 2))),
        "hist_values": gaussian(splits[4], (HISTORY, D), 1.0, 6.0, ((0, 16), (1, 2))),
        "piece_readers": draw_piece_readers(jax.random.fold_in(splits[7], 71), 0),
        "out_weight": gaussian(splits[6], (D, D), (D // 16) ** -0.5, 0.3125, ((0, 2),)),
    }


def reference(queries, cur_keys, cur_values, hist_keys, hist_values, piece_readers, out_weight):
    scale = 1.0 / math.sqrt(HDIM)
    query_blocks = queries.reshape(READERS, TOK_DEV, HEADS, HDIM)
    key_cur = cur_keys.astype(jnp.float32).reshape(TOKENS, HEADS, HDIM)
    val_cur = cur_values.astype(jnp.float32).reshape(TOKENS, HEADS, HDIM)
    key_hist = hist_keys.astype(jnp.float32).reshape(HISTORY, HEADS, HDIM)
    val_hist = hist_values.astype(jnp.float32).reshape(HISTORY, HEADS, HDIM)
    reader_ids = jnp.arange(READERS, dtype=jnp.int32)
    routed = jnp.any(piece_readers[None, :, :] == reader_ids[:, None, None], axis=2)
    key_masks = jnp.repeat(routed, PIECE, axis=1)

    def one_block(pair):
        query_rows, live_keys = pair
        query_f = query_rows.astype(jnp.float32)
        score_cur = jnp.einsum('qhd,khd->hqk', query_f, key_cur) * scale
        score_hist = jnp.einsum('qhd,khd->hqk', query_f, key_hist) * scale
        score_hist = jnp.where(live_keys[None, None, :], score_hist, -1e+30)
        row_max = jnp.maximum(lax.optimization_barrier(jnp.max(score_cur, axis=-1)), lax.optimization_barrier(jnp.max(score_hist, axis=-1)))
        expo_cur = jnp.exp(score_cur - row_max[..., None])
        expo_hist = jnp.where(live_keys[None, None, :], jnp.exp(score_hist - row_max[..., None]), 0.0)
        total = lax.optimization_barrier(jnp.sum(expo_cur, axis=-1)) + lax.optimization_barrier(jnp.sum(expo_hist, axis=-1))
        weight_cur = lax.optimization_barrier(expo_cur.astype(jnp.bfloat16)).astype(jnp.float32)
        weight_hist = lax.optimization_barrier(expo_hist.astype(jnp.bfloat16)).astype(jnp.float32)
        summed = jnp.einsum('hqk,khd->qhd', weight_cur, val_cur) + jnp.einsum('hqk,khd->qhd', weight_hist, val_hist)
        result = summed / jnp.transpose(total)[:, :, None]
        return result.astype(jnp.bfloat16).reshape(TOK_DEV, D)
    attended = lax.map(one_block, (query_blocks, key_masks)).reshape(TOKENS, D)
    return jnp.dot(attended, out_weight, preferred_element_type=jnp.float32).astype(jnp.bfloat16)
```

```python
import functools
import math

import jax
import jax.numpy as jnp
from jax import lax
from jax.experimental import pallas as pl
from jax.experimental.pallas import tpu as pltpu
from jax.sharding import PartitionSpec as P

HDIM = 128
CAP = 2
PLANE = 4
LOG2 = math.log2(math.e) / math.sqrt(HDIM)
MESH = pl.DeviceIdType.MESH
F32 = jnp.float32
BF16 = jnp.bfloat16
NT = (((1,), (1,)), ((), ()))
TN = (((0,), (0,)), ((), ()))


def kernel(nz, chunks, hc, piece, sel, q_in, k_in, v_in, hk_in, hv_in, out,
           qx, kb, vb, hkb, hvb, hkw, hvw, ocs, mls, ocr, mlr, r, rml, zlb, zlml, zrb, zrml, fb, bias,
           q_loc, q_xs, q_xr, kv_loc, kv_xs, kv_xr,
           qc_s, qc_r, qr_s, qr_r, ql_s, ql_r,
           oc_s, oc_r, om_s, om_r, zl_s, zl_r, zlm_s, zlm_r, zr_s, zr_r, zrm_s, zrm_r,
           f_loc, f_s, f_r):
    s = lax.axis_index("seq")
    hd = lax.axis_index("head")
    z, x, c = s // PLANE, (s // 2) % 2, s % 2
    tok = q_in.shape[0]
    both = 2 * tok
    w = hc * HDIM
    half = chunks * w
    xp = (z * PLANE + (1 - x) * 2 + c, hd)
    cp = (z * PLANE + x * 2 + (1 - c), hd)
    left = (jnp.maximum(s - PLANE, 0), hd)
    right = (jnp.minimum(s + PLANE, nz * PLANE - 1), hd)
    has_left, has_right = z > 0, z < nz - 1
    own = z * 2 + c

    def remote(src, dst, ss, rs, dev):
        return pltpu.make_async_remote_copy(
            src_ref=src, dst_ref=dst, send_sem=ss, recv_sem=rs, device_id=dev, device_id_type=MESH)

    def cols(side, k):
        return pl.ds(pl.multiple_of(side * half + k * w, HDIM), w)

    def q_own(k):
        return pltpu.make_async_copy(q_in.at[:, cols(x, k)], qx.at[own, k, x], q_loc.at[k])

    def q_cross(k):
        return remote(q_in.at[:, cols(1 - x, k)], qx.at[own, k, x], q_xs.at[k], q_xr.at[k], xp)

    pairs = ((k_in, kb), (v_in, vb), (hk_in, hkb), (hv_in, hvb))

    def kv_own(k, i):
        return pltpu.make_async_copy(pairs[i][0].at[:, cols(x, k)], pairs[i][1].at[k, 0], kv_loc.at[i, k])

    def kv_cross(k, i):
        return remote(pairs[i][0].at[:, cols(1 - x, k)], pairs[i][1].at[k, 1], kv_xs.at[i, k], kv_xr.at[i, k], xp)

    def kv_start(k):
        for i in range(4):
            kv_own(k, i).start()
            kv_cross(k, i).start()

    def q_to(zs, k, which):
        ss, rs, dev = {"c": (qc_s, qc_r, cp), "r": (qr_s, qr_r, right), "l": (ql_s, ql_r, left)}[which]
        slot = zs * 2 + c
        return remote(qx.at[slot, k], qx.at[slot, k], ss.at[zs, k], rs.at[zs, k], dev)

    def q_hop1(k):
        q_own(k).wait()
        q_cross(k).wait_recv()

        @pl.when(has_right)
        def _():
            q_to(z, k, "r").start()

        @pl.when(has_left)
        def _():
            q_to(z, k, "l").start()

        q_to(z, k, "c").start()

    def q_forward(k, d):
        @pl.when(z - d >= 0)
        def _():
            q_to(z - d, k, "r").wait_recv()

            @pl.when(has_right)
            def _():
                q_to(z - d, k, "r").start()

            q_to(z - d, k, "c").start()

        @pl.when(z + d < nz)
        def _():
            q_to(z + d, k, "l").wait_recv()

            @pl.when(has_left)
            def _():
                q_to(z + d, k, "l").start()

            q_to(z + d, k, "c").start()

    def o_core(t, k):
        return (remote(ocs.at[t, k], ocr.at[t, k], oc_s.at[t, k], oc_r.at[t, k], cp),
                remote(mls.at[t, k], mlr.at[t, k], om_s.at[t, k], om_r.at[t, k], cp))

    def o_right(t, k):
        return (remote(r.at[t, k], zlb.at[t, k], zl_s.at[t, k], zl_r.at[t, k], right),
                remote(rml.at[t, k], zlml.at[t, k], zlm_s.at[t, k], zlm_r.at[t, k], right))

    def o_left(t, k):
        return (remote(r.at[t, k], zrb.at[t, k], zr_s.at[t, k], zr_r.at[t, k], left),
                remote(rml.at[t, k], zrml.at[t, k], zrm_s.at[t, k], zrm_r.at[t, k], left))

    def get(o_ref, ml_ref, t, k, h):
        return (o_ref[t, k, h * HDIM:(h + 1) * HDIM, :].astype(F32),
                ml_ref[t, k, h * 8:h * 8 + 1, :], ml_ref[t, k, h * 8 + 1:h * 8 + 2, :])

    def put(o_ref, ml_ref, t, k, h, part):
        o, m, l = part
        o_ref[t, k, h * HDIM:(h + 1) * HDIM, :] = o.astype(BF16)
        row = lax.broadcasted_iota(jnp.int32, (8, both), 0)
        ml_ref[t, k, h * 8:(h + 1) * 8, :] = jnp.where(row == 0, m, l)

    def merge(a, b):
        m = jnp.maximum(a[1], b[1])
        fa, fb_ = jnp.exp2((a[1] - m) * LOG2), jnp.exp2((b[1] - m) * LOG2)
        return a[0] * fa + b[0] * fb_, m, a[2] * fa + b[2] * fb_

    def partial(k, t, cc, h):
        lanes = slice(h * HDIM, (h + 1) * HDIM)
        qs = qx[t * 2 + cc, k, :, :, lanes].reshape(both, HDIM)
        kc = kb[k, :, :, lanes].reshape(both, HDIM)
        vc = vb[k, :, :, lanes].reshape(both, HDIM)
        kh, vh = [], []
        for xx in range(2):
            b = t * PLANE + xx * 2 + cc
            for src in range(2):
                for slot in range(CAP):
                    n = sel[b, src * 4 + slot]
                    kh.append(hkw[src, n, :, lanes])
                    vh.append(hvw[src, n, :, lanes])
        kh, vh = jnp.concatenate(kh, axis=0), jnp.concatenate(vh, axis=0)
        s1 = lax.dot_general(kc, qs, NT, preferred_element_type=F32)
        s2 = lax.dot_general(kh, qs, NT, preferred_element_type=F32) + bias[t * 2 + cc]
        m = jnp.maximum(jnp.max(s1, axis=0, keepdims=True), jnp.max(s2, axis=0, keepdims=True))
        p1 = jnp.exp2((s1 - m) * LOG2)
        p2 = jnp.exp2((s2 - m) * LOG2)
        l = jnp.sum(p1, axis=0, keepdims=True) + jnp.sum(p2, axis=0, keepdims=True)
        o = lax.dot_general(vc, p1.astype(BF16), TN, preferred_element_type=F32)
        o = o + lax.dot_general(vh, p2.astype(BF16), TN, preferred_element_type=F32)
        return o, m, l

    def rs_step(k, wave):
        @pl.when((z == wave) & has_right)
        def _():
            def one(i, _):
                t = nz - 1 - i

                @pl.when(t > z)
                def _():
                    @pl.when(has_left)
                    def _():
                        for cpy in o_right(t, k):
                            cpy.wait_recv()
                        for h in range(hc):
                            put(r, rml, t, k, h, merge(get(r, rml, t, k, h), get(zlb, zlml, t, k, h)))
                    for cpy in o_right(t, k):
                        cpy.start()
                return 0
            lax.fori_loop(0, nz, one, 0)

        @pl.when((z == nz - 1 - wave) & has_left)
        def _():
            def one(t, _):
                @pl.when(t < z)
                def _():
                    @pl.when(has_right)
                    def _():
                        for cpy in o_left(t, k):
                            cpy.wait_recv()
                        for h in range(hc):
                            put(r, rml, t, k, h, merge(get(r, rml, t, k, h), get(zrb, zrml, t, k, h)))
                    for cpy in o_left(t, k):
                        cpy.start()
                return 0
            lax.fori_loop(0, nz, one, 0)

    def final_own(k):
        return pltpu.make_async_copy(fb.at[k, x], out.at[:, cols(x, k)], f_loc.at[k])

    def final_cross(k):
        return remote(fb.at[k, 1 - x], out.at[:, cols(x, k)], f_s.at[k], f_r.at[k], xp)

    def final(k):
        @pl.when(has_left)
        def _():
            for cpy in o_right(z, k):
                cpy.wait_recv()
            for h in range(hc):
                put(r, rml, z, k, h, merge(get(r, rml, z, k, h), get(zlb, zlml, z, k, h)))

        @pl.when(has_right)
        def _():
            for cpy in o_left(z, k):
                cpy.wait_recv()
            for h in range(hc):
                put(r, rml, z, k, h, merge(get(r, rml, z, k, h), get(zrb, zrml, z, k, h)))

        for h in range(hc):
            o, _, l = get(r, rml, z, k, h)
            done = jnp.transpose(o / l).astype(BF16)
            fb[k, :, :, h * HDIM:(h + 1) * HDIM] = done.reshape(2, tok, HDIM)
        final_own(k).start()
        final_cross(k).start()

    barrier = pltpu.get_barrier_semaphore()
    for dev in (xp, cp):
        pl.semaphore_signal(barrier, inc=1, device_id=dev, device_id_type=MESH)

    @pl.when(has_left)
    def _():
        pl.semaphore_signal(barrier, inc=1, device_id=left, device_id_type=MESH)

    @pl.when(has_right)
    def _():
        pl.semaphore_signal(barrier, inc=1, device_id=right, device_id_type=MESH)

    pl.semaphore_wait(barrier, 2 + has_left.astype(jnp.int32) + has_right.astype(jnp.int32))

    for k in range(chunks):
        q_cross(k).start()
        q_own(k).start()
    for k in range(min(2, chunks)):
        kv_start(k)

    block_of = lax.broadcasted_iota(jnp.int32, (piece, both), 1) // tok

    def fill(i, _):
        t, cc = i // 2, i % 2
        for xx in range(2):
            b = t * PLANE + xx * 2 + cc
            for src in range(2):
                for slot in range(CAP):
                    n = (xx * 2 + src) * CAP + slot
                    live = (sel[b, src * 4 + CAP + slot].astype(F32) - 1.0) * 1e30
                    bias[i, n * piece:(n + 1) * piece, :] = jnp.where(block_of == xx, live, -1e30)
        return 0

    lax.fori_loop(0, nz * 2, fill, 0)

    for k in range(min(2, chunks)):
        q_hop1(k)
    for d in range(1, nz):
        q_forward(0, d)

    def slot_body(j, _):
        k, second = j // 2, j % 2

        @pl.when((k < chunks) & (second == 0))
        def _():
            for i in range(4):
                kv_own(k, i).wait()
                kv_cross(k, i).wait_recv()

            @pl.when(k + 2 < chunks)
            def _():
                kv_start(k + 2)
                q_hop1(k + 2)
            hkw[...] = hkb[k].reshape(hkw.shape)
            hvw[...] = hvb[k].reshape(hvw.shape)

            def got(zs, _):
                q_to(zs, k, "c").wait_recv()
                return 0
            lax.fori_loop(0, nz, got, 0)

        @pl.when((k + 1 < chunks) & (second == 0))
        def _():
            q_forward(k + 1, 1)

        @pl.when((k + 1 < chunks) & (second == 1))
        def _():
            for d in range(2, nz):
                q_forward(k + 1, d)

        @pl.when(k < chunks)
        def _():
            cc = jnp.where(second == 0, 1 - c, c)

            def target(t, _):
                parts = [partial(k, t, cc, h) for h in range(hc)]

                @pl.when(second == 0)
                def _():
                    for h in range(hc):
                        put(ocs, mls, t, k, h, parts[h])
                    for cpy in o_core(t, k):
                        cpy.start()

                @pl.when(second == 1)
                def _():
                    for cpy in o_core(t, k):
                        cpy.wait_recv()
                    for h in range(hc):
                        put(r, rml, t, k, h, merge(parts[h], get(ocr, mlr, t, k, h)))
                return 0
            lax.fori_loop(0, nz, target, 0)

        def waves(i, _):
            wave = nz - 1 - i
            age = j - 1 - wave
            kk = age // 2

            @pl.when((age >= 0) & (age % 2 == 0) & (kk < chunks))
            def _():
                rs_step(kk, wave)

                @pl.when(wave == nz - 1)
                def _():
                    final(kk)
            return 0
        lax.fori_loop(0, nz, waves, 0)
        return 0

    lax.fori_loop(0, 2 * chunks + nz, slot_body, 0)

    def drain(k, _):
        q_cross(k).wait_send()
        for i in range(4):
            kv_cross(k, i).wait_send()
        final_own(k).wait()
        final_cross(k).wait()

        def each(t, _):
            q_to(t, k, "c").wait_send()
            for cpy in o_core(t, k):
                cpy.wait_send()

            @pl.when(has_right & (t <= z))
            def _():
                q_to(t, k, "r").wait_send()

            @pl.when(has_left & (t >= z))
            def _():
                q_to(t, k, "l").wait_send()

            @pl.when(t > z)
            def _():
                for cpy in o_right(t, k):
                    cpy.wait_send()

            @pl.when(t < z)
            def _():
                for cpy in o_left(t, k):
                    cpy.wait_send()
            return 0
        lax.fori_loop(0, nz, each, 0)
        return 0

    lax.fori_loop(0, chunks, drain, 0)


def reader_table(piece_readers, readers):
    hits = jnp.any(piece_readers[:, :, None] == jnp.arange(readers, dtype=jnp.int32)[None, None, :], axis=1)
    hits = hits.astype(jnp.int32)
    rank = jnp.cumsum(hits, axis=0) - hits
    index = jnp.arange(piece_readers.shape[0], dtype=jnp.int32)[:, None]
    where = [jnp.sum(jnp.where((hits > 0) & (rank == n), index, 0), axis=0) for n in range(CAP)]
    count = jnp.sum(hits, axis=0)
    return jnp.stack(where + [(count > n).astype(jnp.int32) for n in range(CAP)], axis=1)


def fused_attention(queries, cur_keys, cur_values, hist_keys, hist_values, piece_readers):
    tok, width = queries.shape
    hist = hist_keys.shape[0]
    readers = lax.axis_size("seq")
    nz = readers // PLANE
    half_heads = width // HDIM // 2
    hc = 2 if half_heads % 2 == 0 else 1
    chunks = half_heads // hc
    w = hc * HDIM
    both = 2 * tok
    piece = hist // piece_readers.shape[0]
    table = reader_table(piece_readers, readers)
    other = lax.ppermute(table, "seq", [(i, i ^ 2) for i in range(readers)])
    sel = jnp.concatenate([table, other], axis=1)
    vm = pltpu.VMEM
    sem = pltpu.SemaphoreType.DMA
    o_buf = vm((nz, chunks, w, both), BF16)
    ml_buf = vm((nz, chunks, hc * 8, both), F32)
    scratch = [
        vm((nz * 2, chunks, 2, tok, w), BF16),
        vm((chunks, 2, tok, w), BF16), vm((chunks, 2, tok, w), BF16),
        vm((chunks, 2, hist, w), BF16), vm((chunks, 2, hist, w), BF16),
        vm((2, hist // piece, piece, w), BF16), vm((2, hist // piece, piece, w), BF16),
        o_buf, ml_buf, o_buf, ml_buf, o_buf, ml_buf, o_buf, ml_buf, o_buf, ml_buf,
        vm((chunks, 2, tok, w), BF16),
        vm((nz * 2, 4 * CAP * piece, both), F32),
    ]
    scratch += [sem((chunks,))] * 3 + [sem((4, chunks))] * 3 + [sem((nz, chunks))] * 18 + [sem((chunks,))] * 3
    any_spec = pl.BlockSpec(memory_space=pl.ANY)
    flops = 4 * readers * tok * (2 * tok + 4 * CAP * piece) * width // 2
    return pl.pallas_call(
        functools.partial(kernel, nz, chunks, hc, piece),
        out_shape=jax.ShapeDtypeStruct((tok, width), BF16),
        in_specs=[pl.BlockSpec(memory_space=pltpu.SMEM)] + [any_spec] * 5,
        out_specs=any_spec,
        scratch_shapes=scratch,
        compiler_params=pltpu.CompilerParams(
            collective_id=0, has_side_effects=True, vmem_limit_bytes=60 * 1024 * 1024),
        cost_estimate=pl.CostEstimate(flops=flops, bytes_accessed=12 * tok * width, transcendentals=flops // 512),
    )(sel, queries, cur_keys, cur_values, hist_keys, hist_values)


def local_fused(queries, cur_keys, cur_values, hist_keys, hist_values, piece_readers, out_weight):
    attended = fused_attention(queries, cur_keys, cur_values, hist_keys, hist_values, piece_readers)
    partial_out = jnp.dot(attended, out_weight, preferred_element_type=F32)
    return lax.psum_scatter(partial_out.astype(BF16), "head", scatter_dimension=1, tiled=True)


def passed_along(value, axis, by):
    length = lax.axis_size(axis)
    return lax.ppermute(value, axis, [(i, (i + by) % length) for i in range(length)])


def attend(totals, query_heads, key_val, valid_keys):
    run_max, run_num, run_sum = totals
    head_count = query_heads.shape[1]
    key_heads = key_val[0].reshape(-1, head_count, HDIM)
    val_heads = key_val[1].reshape(-1, head_count, HDIM)
    scores = jnp.einsum("qhd,khd->hqk", query_heads, key_heads, preferred_element_type=jnp.float32)
    scores = scores * (1.0 / math.sqrt(HDIM))
    if valid_keys is not None:
        scores = jnp.where(valid_keys[None, None, :], scores, -1e30)
    new_max = jnp.maximum(run_max, jnp.max(scores, axis=-1))
    weights = jnp.exp(scores - new_max[..., None])
    if valid_keys is not None:
        weights = jnp.where(valid_keys[None, None, :], weights, 0.0)
    fade_by = jnp.exp(run_max - new_max)
    product = jnp.einsum(
        "hqk,khd->hqd", weights.astype(jnp.bfloat16), val_heads, preferred_element_type=jnp.float32
    )
    run_num = run_num * fade_by[..., None] + product
    run_sum = run_sum * fade_by + jnp.sum(weights, axis=-1)
    return (new_max, run_num, run_sum)


def local(queries, cur_keys, cur_values, hist_keys, hist_values, piece_readers, out_weight):
    tok_rows = queries.shape[0]
    width = queries.shape[1]
    head_count = width // HDIM
    query_heads = queries.reshape(tok_rows, head_count, HDIM)
    reader_count = lax.axis_size("seq")
    owner_rows = piece_readers.shape[0]
    piece_len = hist_keys.shape[0] // owner_rows
    reader_ids = jnp.arange(reader_count, dtype=jnp.int32)
    hits = jnp.sum(
        (piece_readers[:, :, None] == reader_ids[None, None, :]).astype(jnp.int32), axis=1
    )
    earlier = jnp.cumsum(hits, axis=0) - hits
    slot_ids = jnp.arange(CAP, dtype=jnp.int32)
    select = hits[None, :, :] * (earlier[None, :, :] == slot_ids[:, None, None]).astype(jnp.int32)
    select = jnp.transpose(select, (2, 0, 1))
    slot_full = jnp.sum(select, axis=2)[None, :, :]
    stacked = jnp.stack([hist_keys, hist_values]).reshape(2, owner_rows, piece_len * width)
    outgoing = jnp.einsum(
        "rcp,spx->srcx", select.astype(jnp.bfloat16), stacked, preferred_element_type=jnp.float32
    ).astype(jnp.bfloat16)
    arrived, arrived_full = (
        lax.all_to_all(outgoing, "seq", split_axis=1, concat_axis=1, tiled=True),
        lax.all_to_all(slot_full, "seq", split_axis=1, concat_axis=1, tiled=True),
    )
    hist_kv = arrived.reshape(2, -1, width)
    valid_keys = jnp.repeat(arrived_full.reshape(-1), piece_len) > 0
    start_totals = (
        jnp.full((head_count, tok_rows), -1e30, jnp.float32),
        jnp.zeros((head_count, tok_rows, HDIM), jnp.float32),
        jnp.zeros((head_count, tok_rows), jnp.float32),
    )
    totals = attend(start_totals, query_heads, hist_kv, valid_keys)
    own_block = jnp.stack([cur_keys, cur_values])
    totals = attend(totals, query_heads, own_block, None)

    def cycle_turn(step_idx, loop_state):
        travel, inner = loop_state
        travel = passed_along(travel, "seq", 1)
        return (travel, attend(inner, query_heads, travel, None))

    travel_end, totals = lax.fori_loop(0, reader_count - 1, cycle_turn, (own_block, totals))
    run_max, run_num, run_sum = totals
    attended = run_num / run_sum[..., None]
    attended = jnp.transpose(attended, (1, 0, 2)).reshape(tok_rows, width).astype(jnp.bfloat16)
    partial_out = jnp.dot(attended, out_weight, preferred_element_type=jnp.float32)
    return lax.psum_scatter(
        partial_out.astype(jnp.bfloat16), "head", scatter_dimension=1, tiled=True
    )


def solution(mesh):
    placed = (
        P("seq", "head"),
        P("seq", "head"),
        P("seq", "head"),
        P("seq", "head"),
        P("seq", "head"),
        P("seq", None),
        P("head", None),
    )

    def run(*args):
        heads = args[0].shape[1] // mesh.shape["head"] // HDIM
        whole_planes = mesh.shape["seq"] % PLANE == 0 and heads % 2 == 0
        return jax.shard_map(
            local_fused if whole_planes else local,
            mesh=mesh, in_specs=placed, out_specs=P("seq", "head"), check_vma=False,
        )(*args)

    return run
```

```python
import functools
import math

import jax
import jax.numpy as jnp
from jax import lax
from jax.experimental import pallas as pl
from jax.experimental.pallas import tpu as pltpu
from jax.sharding import PartitionSpec as P

HDIM = 128
CAP = 2
PLANE = 4
LOG2 = math.log2(math.e) / math.sqrt(HDIM)
MESH = pl.DeviceIdType.MESH
F32 = jnp.float32
BF16 = jnp.bfloat16
NT = (((1,), (1,)), ((), ()))
TN = (((0,), (0,)), ((), ()))


def kernel(nz, chunks, hc, piece, sel, q_in, k_in, v_in, hk_in, hv_in, w_in, out,
           qx, kb, vb, hkb, hvb, hkw, hvw, ocs, mls, ocr, mlr, r, rml, zlb, zlml, zrb, zrml, fs, att, bias,
           wbuf, acc, ysend, yrecv,
           q_loc, q_xs, q_xr, kv_loc, kv_xs, kv_xr,
           qc_s, qc_r, qr_s, qr_r, ql_s, ql_r,
           oc_s, oc_r, om_s, om_r, zl_s, zl_r, zlm_s, zlm_r, zr_s, zr_r, zrm_s, zrm_r,
           w_sem, f_s, f_r, y_s, y_r):
    s = lax.axis_index("seq")
    hd = lax.axis_index("head")
    z, x, c = s // PLANE, (s // 2) % 2, s % 2
    tok = q_in.shape[0]
    both = 2 * tok
    w = hc * HDIM
    half = chunks * w
    xp = (z * PLANE + (1 - x) * 2 + c, hd)
    cp = (z * PLANE + x * 2 + (1 - c), hd)
    left = (jnp.maximum(s - PLANE, 0), hd)
    right = (jnp.minimum(s + PLANE, nz * PLANE - 1), hd)
    yp = (s, 1 - hd)
    tiles, _, tile = ysend.shape
    has_left, has_right = z > 0, z < nz - 1
    own = z * 2 + c

    def remote(src, dst, ss, rs, dev):
        return pltpu.make_async_remote_copy(
            src_ref=src, dst_ref=dst, send_sem=ss, recv_sem=rs, device_id=dev, device_id_type=MESH)

    def cols(side, k):
        return pl.ds(pl.multiple_of(side * half + k * w, HDIM), w)

    def q_own(k):
        return pltpu.make_async_copy(q_in.at[:, cols(x, k)], qx.at[own, k, x], q_loc.at[k])

    def q_cross(k):
        return remote(q_in.at[:, cols(1 - x, k)], qx.at[own, k, x], q_xs.at[k], q_xr.at[k], xp)

    pairs = ((k_in, kb), (v_in, vb), (hk_in, hkb), (hv_in, hvb))

    def kv_own(k, i):
        return pltpu.make_async_copy(pairs[i][0].at[:, cols(x, k)], pairs[i][1].at[k, 0], kv_loc.at[i, k])

    def kv_cross(k, i):
        return remote(pairs[i][0].at[:, cols(1 - x, k)], pairs[i][1].at[k, 1], kv_xs.at[i, k], kv_xr.at[i, k], xp)

    def kv_start(k):
        for i in range(4):
            kv_own(k, i).start()
            kv_cross(k, i).start()

    def q_to(zs, k, which):
        ss, rs, dev = {"c": (qc_s, qc_r, cp), "r": (qr_s, qr_r, right), "l": (ql_s, ql_r, left)}[which]
        slot = zs * 2 + c
        return remote(qx.at[slot, k], qx.at[slot, k], ss.at[zs, k], rs.at[zs, k], dev)

    def q_hop1(k):
        q_own(k).wait()
        q_cross(k).wait_recv()

        @pl.when(has_right)
        def _():
            q_to(z, k, "r").start()

        @pl.when(has_left)
        def _():
            q_to(z, k, "l").start()

        q_to(z, k, "c").start()

    def q_forward(k, d):
        @pl.when(z - d >= 0)
        def _():
            q_to(z - d, k, "r").wait_recv()

            @pl.when(has_right)
            def _():
                q_to(z - d, k, "r").start()

            q_to(z - d, k, "c").start()

        @pl.when(z + d < nz)
        def _():
            q_to(z + d, k, "l").wait_recv()

            @pl.when(has_left)
            def _():
                q_to(z + d, k, "l").start()

            q_to(z + d, k, "c").start()

    def o_core(t, k):
        return (remote(ocs.at[t, k], ocr.at[t, k], oc_s.at[t, k], oc_r.at[t, k], cp),
                remote(mls.at[t, k], mlr.at[t, k], om_s.at[t, k], om_r.at[t, k], cp))

    def o_right(t, k):
        return (remote(r.at[t, k], zlb.at[t, k], zl_s.at[t, k], zl_r.at[t, k], right),
                remote(rml.at[t, k], zlml.at[t, k], zlm_s.at[t, k], zlm_r.at[t, k], right))

    def o_left(t, k):
        return (remote(r.at[t, k], zrb.at[t, k], zr_s.at[t, k], zr_r.at[t, k], left),
                remote(rml.at[t, k], zrml.at[t, k], zrm_s.at[t, k], zrm_r.at[t, k], left))

    def get(o_ref, ml_ref, t, k, h):
        return (o_ref[t, k, h * HDIM:(h + 1) * HDIM, :].astype(F32),
                ml_ref[t, k, h * 8:h * 8 + 1, :], ml_ref[t, k, h * 8 + 1:h * 8 + 2, :])

    def put(o_ref, ml_ref, t, k, h, part):
        o, m, l = part
        o_ref[t, k, h * HDIM:(h + 1) * HDIM, :] = o.astype(BF16)
        row = lax.broadcasted_iota(jnp.int32, (8, both), 0)
        ml_ref[t, k, h * 8:(h + 1) * 8, :] = jnp.where(row == 0, m, l)

    def merge(a, b):
        m = jnp.maximum(a[1], b[1])
        fa, fb_ = jnp.exp2((a[1] - m) * LOG2), jnp.exp2((b[1] - m) * LOG2)
        return a[0] * fa + b[0] * fb_, m, a[2] * fa + b[2] * fb_

    def partial(k, t, cc, h):
        lanes = slice(h * HDIM, (h + 1) * HDIM)
        qs = qx[t * 2 + cc, k, :, :, lanes].reshape(both, HDIM)
        kc = kb[k, :, :, lanes].reshape(both, HDIM)
        vc = vb[k, :, :, lanes].reshape(both, HDIM)
        kh, vh = [], []
        for xx in range(2):
            b = t * PLANE + xx * 2 + cc
            for src in range(2):
                for slot in range(CAP):
                    n = sel[b, src * 4 + slot]
                    kh.append(hkw[src, n, :, lanes])
                    vh.append(hvw[src, n, :, lanes])
        kh, vh = jnp.concatenate(kh, axis=0), jnp.concatenate(vh, axis=0)
        s1 = lax.dot_general(kc, qs, NT, preferred_element_type=F32)
        s2 = lax.dot_general(kh, qs, NT, preferred_element_type=F32) + bias[t * 2 + cc]
        m = jnp.maximum(jnp.max(s1, axis=0, keepdims=True), jnp.max(s2, axis=0, keepdims=True))
        p1 = jnp.exp2((s1 - m) * LOG2)
        p2 = jnp.exp2((s2 - m) * LOG2)
        l = jnp.sum(p1, axis=0, keepdims=True) + jnp.sum(p2, axis=0, keepdims=True)
        o = lax.dot_general(vc, p1.astype(BF16), TN, preferred_element_type=F32)
        o = o + lax.dot_general(vh, p2.astype(BF16), TN, preferred_element_type=F32)
        return o, m, l

    def rs_step(k, wave):
        @pl.when((z == wave) & has_right)
        def _():
            def one(i, _):
                t = nz - 1 - i

                @pl.when(t > z)
                def _():
                    @pl.when(has_left)
                    def _():
                        for cpy in o_right(t, k):
                            cpy.wait_recv()
                        for h in range(hc):
                            put(r, rml, t, k, h, merge(get(r, rml, t, k, h), get(zlb, zlml, t, k, h)))
                    for cpy in o_right(t, k):
                        cpy.start()
                return 0
            lax.fori_loop(0, nz, one, 0)

        @pl.when((z == nz - 1 - wave) & has_left)
        def _():
            def one(t, _):
                @pl.when(t < z)
                def _():
                    @pl.when(has_right)
                    def _():
                        for cpy in o_left(t, k):
                            cpy.wait_recv()
                        for h in range(hc):
                            put(r, rml, t, k, h, merge(get(r, rml, t, k, h), get(zrb, zrml, t, k, h)))
                    for cpy in o_left(t, k):
                        cpy.start()
                return 0
            lax.fori_loop(0, nz, one, 0)

    def final_cross(k):
        return remote(fs.at[k], att.at[x, k], f_s.at[k], f_r.at[k], xp)

    def w_fetch(k, side):
        rows = pl.ds(pl.multiple_of(side * half + k * w, HDIM), w)
        return pltpu.make_async_copy(w_in.at[rows], wbuf.at[k % 2, side], w_sem.at[side, k])

    def y_cross(i):
        return remote(ysend.at[i], yrecv.at[i], y_s.at[i], y_r.at[i], yp)

    def project(k):
        final_cross(k).wait_recv()
        for side in range(2):
            w_fetch(k, side).wait()
        a = jnp.concatenate([att[0, k], att[1, k]], axis=1)

        def one(i, _):
            lanes = pl.ds(pl.multiple_of(((1 - hd) * tiles + i) % (2 * tiles) * tile, tile), tile)
            b = wbuf[k % 2, :, :, lanes].reshape(2 * w, tile)
            value = acc[:, lanes] + jnp.dot(a, b, preferred_element_type=F32)
            acc[:, lanes] = value

            @pl.when((k == chunks - 1) & (i < tiles))
            def _():
                ysend[i] = value.astype(BF16)
                y_cross(i).start()
            return 0
        lax.fori_loop(0, 2 * tiles, one, 0)

        @pl.when(k + 2 < chunks)
        def _():
            for side in range(2):
                w_fetch(k + 2, side).start()

    def final(k):
        @pl.when(has_left)
        def _():
            for cpy in o_right(z, k):
                cpy.wait_recv()
            for h in range(hc):
                put(r, rml, z, k, h, merge(get(r, rml, z, k, h), get(zlb, zlml, z, k, h)))

        @pl.when(has_right)
        def _():
            for cpy in o_left(z, k):
                cpy.wait_recv()
            for h in range(hc):
                put(r, rml, z, k, h, merge(get(r, rml, z, k, h), get(zrb, zrml, z, k, h)))

        for h in range(hc):
            o, _, l = get(r, rml, z, k, h)
            done = jnp.transpose(o / l).astype(BF16)
            lanes = slice(h * HDIM, (h + 1) * HDIM)
            mine, theirs = done[:tok], done[tok:]
            att[x, k, :, lanes] = jnp.where(x == 0, mine, theirs)
            fs[k, :, lanes] = jnp.where(x == 0, theirs, mine)
        final_cross(k).start()

    barrier = pltpu.get_barrier_semaphore()
    for dev in (xp, cp, yp):
        pl.semaphore_signal(barrier, inc=1, device_id=dev, device_id_type=MESH)

    @pl.when(has_left)
    def _():
        pl.semaphore_signal(barrier, inc=1, device_id=left, device_id_type=MESH)

    @pl.when(has_right)
    def _():
        pl.semaphore_signal(barrier, inc=1, device_id=right, device_id_type=MESH)

    pl.semaphore_wait(barrier, 3 + has_left.astype(jnp.int32) + has_right.astype(jnp.int32))

    for k in range(chunks):
        q_cross(k).start()
        q_own(k).start()
    for k in range(min(2, chunks)):
        kv_start(k)
    for k in range(min(2, chunks)):
        for side in range(2):
            w_fetch(k, side).start()
    acc[...] = jnp.zeros_like(acc)

    block_of = lax.broadcasted_iota(jnp.int32, (piece, both), 1) // tok

    def fill(i, _):
        t, cc = i // 2, i % 2
        for xx in range(2):
            b = t * PLANE + xx * 2 + cc
            for src in range(2):
                for slot in range(CAP):
                    n = (xx * 2 + src) * CAP + slot
                    live = (sel[b, src * 4 + CAP + slot].astype(F32) - 1.0) * 1e30
                    bias[i, n * piece:(n + 1) * piece, :] = jnp.where(block_of == xx, live, -1e30)
        return 0

    lax.fori_loop(0, nz * 2, fill, 0)

    for k in range(min(nz + 1, chunks)):
        q_hop1(k)
    for k in range(min(nz - 1, chunks)):
        for d in range(1, nz - k):
            q_forward(k, d)

    def slot_body(j, _):
        k, second = j // 2, j % 2

        @pl.when((k < chunks) & (second == 0))
        def _():
            for i in range(4):
                kv_own(k, i).wait()
                kv_cross(k, i).wait_recv()

            @pl.when(k + 2 < chunks)
            def _():
                kv_start(k + 2)

            @pl.when(k + nz + 1 < chunks)
            def _():
                q_hop1(k + nz + 1)

            for d in range(1, nz):
                @pl.when(k + nz - d < chunks)
                def _():
                    q_forward(k + nz - d, d)
            hkw[...] = hkb[k].reshape(hkw.shape)
            hvw[...] = hvb[k].reshape(hvw.shape)

            def got(zs, _):
                q_to(zs, k, "c").wait_recv()
                return 0
            lax.fori_loop(0, nz, got, 0)

        @pl.when(k < chunks)
        def _():
            cc = jnp.where(second == 0, 1 - c, c)

            step = 2 if nz % 2 == 0 else 1

            def target(i, _):
                jobs = [(i * step + u, h) for u in range(step) for h in range(hc)]
                parts = [partial(k, t, cc, h) for t, h in jobs]

                @pl.when(second == 0)
                def _():
                    for (t, h), part in zip(jobs, parts):
                        put(ocs, mls, t, k, h, part)
                    for u in range(step):
                        for cpy in o_core(i * step + u, k):
                            cpy.start()

                @pl.when(second == 1)
                def _():
                    for u in range(step):
                        for cpy in o_core(i * step + u, k):
                            cpy.wait_recv()
                    for (t, h), part in zip(jobs, parts):
                        put(r, rml, t, k, h, merge(part, get(ocr, mlr, t, k, h)))
                return 0
            lax.fori_loop(0, nz // step, target, 0)

        def waves(i, _):
            wave = nz - 1 - i
            age = j - 1 - 2 * wave
            kk = age // 2

            @pl.when((age >= 0) & (age % 2 == 0) & (kk < chunks))
            def _():
                rs_step(kk, wave)

                @pl.when(wave == nz - 1)
                def _():
                    final(kk)
            return 0
        lax.fori_loop(0, nz, waves, 0)
        ready = j - 2 * nz

        @pl.when((ready >= 0) & (ready % 2 == 0))
        def _():
            project(ready // 2)
        return 0

    lax.fori_loop(0, 2 * chunks + 2 * nz - 1, slot_body, 0)

    def finish(i, _):
        y_cross(i).wait_recv()
        lanes = pl.ds(pl.multiple_of((hd * tiles + i) * tile, tile), tile)
        out[:, pl.ds(pl.multiple_of(i * tile, tile), tile)] = (acc[:, lanes] + yrecv[i].astype(F32)).astype(BF16)
        y_cross(i).wait_send()
        return 0

    lax.fori_loop(0, tiles, finish, 0)

    def drain(k, _):
        q_cross(k).wait_send()
        for i in range(4):
            kv_cross(k, i).wait_send()
        final_cross(k).wait_send()

        def each(t, _):
            q_to(t, k, "c").wait_send()
            for cpy in o_core(t, k):
                cpy.wait_send()

            @pl.when(has_right & (t <= z))
            def _():
                q_to(t, k, "r").wait_send()

            @pl.when(has_left & (t >= z))
            def _():
                q_to(t, k, "l").wait_send()

            @pl.when(t > z)
            def _():
                for cpy in o_right(t, k):
                    cpy.wait_send()

            @pl.when(t < z)
            def _():
                for cpy in o_left(t, k):
                    cpy.wait_send()
            return 0
        lax.fori_loop(0, nz, each, 0)
        return 0

    lax.fori_loop(0, chunks, drain, 0)


def reader_table(piece_readers, readers):
    hits = jnp.any(piece_readers[:, :, None] == jnp.arange(readers, dtype=jnp.int32)[None, None, :], axis=1)
    hits = hits.astype(jnp.int32)
    rank = jnp.cumsum(hits, axis=0) - hits
    index = jnp.arange(piece_readers.shape[0], dtype=jnp.int32)[:, None]
    where = [jnp.sum(jnp.where((hits > 0) & (rank == n), index, 0), axis=0) for n in range(CAP)]
    count = jnp.sum(hits, axis=0)
    return jnp.stack(where + [(count > n).astype(jnp.int32) for n in range(CAP)], axis=1)


def local_fused(queries, cur_keys, cur_values, hist_keys, hist_values, piece_readers, out_weight):
    tok, width = queries.shape
    hist = hist_keys.shape[0]
    readers = lax.axis_size("seq")
    nz = readers // PLANE
    half_heads = width // HDIM // 2
    hc = 1
    out_width = out_weight.shape[1]
    tile = 512 if out_width % 1024 == 0 else HDIM
    tiles = out_width // 2 // tile
    chunks = half_heads // hc
    w = hc * HDIM
    both = 2 * tok
    piece = hist // piece_readers.shape[0]
    table = reader_table(piece_readers, readers)
    other = lax.ppermute(table, "seq", [(i, i ^ 2) for i in range(readers)])
    sel = jnp.concatenate([table, other], axis=1)
    vm = pltpu.VMEM
    sem = pltpu.SemaphoreType.DMA
    o_buf = vm((nz, chunks, w, both), BF16)
    ml_buf = vm((nz, chunks, hc * 8, both), F32)
    scratch = [
        vm((nz * 2, chunks, 2, tok, w), BF16),
        vm((chunks, 2, tok, w), BF16), vm((chunks, 2, tok, w), BF16),
        vm((chunks, 2, hist, w), BF16), vm((chunks, 2, hist, w), BF16),
        vm((2, hist // piece, piece, w), BF16), vm((2, hist // piece, piece, w), BF16),
        o_buf, ml_buf, o_buf, ml_buf, o_buf, ml_buf, o_buf, ml_buf, o_buf, ml_buf,
        vm((chunks, tok, w), BF16), vm((2, chunks, tok, w), BF16),
        vm((nz * 2, 4 * CAP * piece, both), F32),
        vm((2, 2, w, out_width), BF16), vm((tok, out_width), F32),
        vm((tiles, tok, tile), BF16), vm((tiles, tok, tile), BF16),
    ]
    scratch += [sem((chunks,))] * 3 + [sem((4, chunks))] * 3 + [sem((nz, chunks))] * 18
    scratch += [sem((2, chunks))] + [sem((chunks,))] * 2 + [sem((tiles,))] * 2
    any_spec = pl.BlockSpec(memory_space=pl.ANY)
    flops = 4 * readers * tok * (2 * tok + 4 * CAP * piece) * width // 2
    return pl.pallas_call(
        functools.partial(kernel, nz, chunks, hc, piece),
        out_shape=jax.ShapeDtypeStruct((tok, out_width // 2), BF16),
        in_specs=[pl.BlockSpec(memory_space=pltpu.SMEM)] + [any_spec] * 6,
        out_specs=pl.BlockSpec(memory_space=pltpu.VMEM),
        scratch_shapes=scratch,
        compiler_params=pltpu.CompilerParams(
            collective_id=0, has_side_effects=True, vmem_limit_bytes=62 * 1024 * 1024),
        cost_estimate=pl.CostEstimate(flops=flops, bytes_accessed=12 * tok * width, transcendentals=flops // 512),
    )(sel, queries, cur_keys, cur_values, hist_keys, hist_values, out_weight)


def passed_along(value, axis, by):
    length = lax.axis_size(axis)
    return lax.ppermute(value, axis, [(i, (i + by) % length) for i in range(length)])


def attend(totals, query_heads, key_val, valid_keys):
    run_max, run_num, run_sum = totals
    head_count = query_heads.shape[1]
    key_heads = key_val[0].reshape(-1, head_count, HDIM)
    val_heads = key_val[1].reshape(-1, head_count, HDIM)
    scores = jnp.einsum("qhd,khd->hqk", query_heads, key_heads, preferred_element_type=jnp.float32)
    scores = scores * (1.0 / math.sqrt(HDIM))
    if valid_keys is not None:
        scores = jnp.where(valid_keys[None, None, :], scores, -1e30)
    new_max = jnp.maximum(run_max, jnp.max(scores, axis=-1))
    weights = jnp.exp(scores - new_max[..., None])
    if valid_keys is not None:
        weights = jnp.where(valid_keys[None, None, :], weights, 0.0)
    fade_by = jnp.exp(run_max - new_max)
    product = jnp.einsum(
        "hqk,khd->hqd", weights.astype(jnp.bfloat16), val_heads, preferred_element_type=jnp.float32
    )
    run_num = run_num * fade_by[..., None] + product
    run_sum = run_sum * fade_by + jnp.sum(weights, axis=-1)
    return (new_max, run_num, run_sum)


def local(queries, cur_keys, cur_values, hist_keys, hist_values, piece_readers, out_weight):
    tok_rows = queries.shape[0]
    width = queries.shape[1]
    head_count = width // HDIM
    query_heads = queries.reshape(tok_rows, head_count, HDIM)
    reader_count = lax.axis_size("seq")
    owner_rows = piece_readers.shape[0]
    piece_len = hist_keys.shape[0] // owner_rows
    reader_ids = jnp.arange(reader_count, dtype=jnp.int32)
    hits = jnp.sum(
        (piece_readers[:, :, None] == reader_ids[None, None, :]).astype(jnp.int32), axis=1
    )
    earlier = jnp.cumsum(hits, axis=0) - hits
    slot_ids = jnp.arange(CAP, dtype=jnp.int32)
    select = hits[None, :, :] * (earlier[None, :, :] == slot_ids[:, None, None]).astype(jnp.int32)
    select = jnp.transpose(select, (2, 0, 1))
    slot_full = jnp.sum(select, axis=2)[None, :, :]
    stacked = jnp.stack([hist_keys, hist_values]).reshape(2, owner_rows, piece_len * width)
    outgoing = jnp.einsum(
        "rcp,spx->srcx", select.astype(jnp.bfloat16), stacked, preferred_element_type=jnp.float32
    ).astype(jnp.bfloat16)
    arrived, arrived_full = (
        lax.all_to_all(outgoing, "seq", split_axis=1, concat_axis=1, tiled=True),
        lax.all_to_all(slot_full, "seq", split_axis=1, concat_axis=1, tiled=True),
    )
    hist_kv = arrived.reshape(2, -1, width)
    valid_keys = jnp.repeat(arrived_full.reshape(-1), piece_len) > 0
    start_totals = (
        jnp.full((head_count, tok_rows), -1e30, jnp.float32),
        jnp.zeros((head_count, tok_rows, HDIM), jnp.float32),
        jnp.zeros((head_count, tok_rows), jnp.float32),
    )
    totals = attend(start_totals, query_heads, hist_kv, valid_keys)
    own_block = jnp.stack([cur_keys, cur_values])
    totals = attend(totals, query_heads, own_block, None)

    def cycle_turn(step_idx, loop_state):
        travel, inner = loop_state
        travel = passed_along(travel, "seq", 1)
        return (travel, attend(inner, query_heads, travel, None))

    travel_end, totals = lax.fori_loop(0, reader_count - 1, cycle_turn, (own_block, totals))
    run_max, run_num, run_sum = totals
    attended = run_num / run_sum[..., None]
    attended = jnp.transpose(attended, (1, 0, 2)).reshape(tok_rows, width).astype(jnp.bfloat16)
    partial_out = jnp.dot(attended, out_weight, preferred_element_type=jnp.float32)
    return lax.psum_scatter(
        partial_out.astype(jnp.bfloat16), "head", scatter_dimension=1, tiled=True
    )


def solution(mesh):
    placed = (
        P("seq", "head"),
        P("seq", "head"),
        P("seq", "head"),
        P("seq", "head"),
        P("seq", "head"),
        P("seq", None),
        P("head", None),
    )

    def run(*args):
        heads = args[0].shape[1] // mesh.shape["head"] // HDIM
        whole_planes = mesh.shape["seq"] % PLANE == 0 and heads % 2 == 0 and mesh.shape["head"] == 2
        return jax.shard_map(
            local_fused if whole_planes else local,
            mesh=mesh, in_specs=placed, out_specs=P("seq", "head"), check_vma=False,
        )(*args)

    return run
```

```python
import functools
import math

import jax
import jax.numpy as jnp
from jax import lax
from jax.experimental import pallas as pl
from jax.experimental.pallas import tpu as pltpu
from jax.sharding import PartitionSpec as P

HDIM = 128
CAP = 2
PLANE = 4
LOG2 = math.log2(math.e) / math.sqrt(HDIM)
MESH = pl.DeviceIdType.MESH
F32 = jnp.float32
BF16 = jnp.bfloat16
NT = (((1,), (1,)), ((), ()))
TN = (((0,), (0,)), ((), ()))


def kernel(nz, chunks, hc, piece, sel, q_in, k_in, v_in, hk_in, hv_in, w_in, out,
           qx, kb, vb, hkb, hvb, hkw, hvw, ocs, mls, ocr, mlr, r, rml, zlb, zlml, zrb, zrml, fs, att, bias, vt,
           wbuf, acc, ysend, yrecv,
           q_loc, q_xs, q_xr, kv_loc, kv_xs, kv_xr,
           qc_s, qc_r, qr_s, qr_r, ql_s, ql_r,
           oc_s, oc_r, om_s, om_r, zl_s, zl_r, zlm_s, zlm_r, zr_s, zr_r, zrm_s, zrm_r,
           w_sem, f_s, f_r, y_s, y_r):
    s = lax.axis_index("seq")
    hd = lax.axis_index("head")
    z, x, c = s // PLANE, (s // 2) % 2, s % 2
    tok = q_in.shape[0]
    both = 2 * tok
    w = hc * HDIM
    half = chunks * w
    xp = (z * PLANE + (1 - x) * 2 + c, hd)
    cp = (z * PLANE + x * 2 + (1 - c), hd)
    left = (jnp.maximum(s - PLANE, 0), hd)
    right = (jnp.minimum(s + PLANE, nz * PLANE - 1), hd)
    yp = (s, 1 - hd)
    tiles, _, tile = ysend.shape
    has_left, has_right = z > 0, z < nz - 1
    own = z * 2 + c

    def remote(src, dst, ss, rs, dev):
        return pltpu.make_async_remote_copy(
            src_ref=src, dst_ref=dst, send_sem=ss, recv_sem=rs, device_id=dev, device_id_type=MESH)

    def cols(side, k):
        return pl.ds(pl.multiple_of(side * half + k * w, HDIM), w)

    def q_own(k):
        return pltpu.make_async_copy(q_in.at[:, cols(x, k)], qx.at[own, k, x], q_loc.at[k])

    def q_cross(k):
        return remote(q_in.at[:, cols(1 - x, k)], qx.at[own, k, x], q_xs.at[k], q_xr.at[k], xp)

    pairs = ((k_in, kb), (v_in, vb), (hk_in, hkb), (hv_in, hvb))

    def kv_own(k, i):
        return pltpu.make_async_copy(pairs[i][0].at[:, cols(x, k)], pairs[i][1].at[k, 0], kv_loc.at[i, k])

    def kv_cross(k, i):
        return remote(pairs[i][0].at[:, cols(1 - x, k)], pairs[i][1].at[k, 1], kv_xs.at[i, k], kv_xr.at[i, k], xp)

    def kv_start(k):
        for i in range(4):
            kv_own(k, i).start()
            kv_cross(k, i).start()

    def q_to(zs, k, which):
        ss, rs, dev = {"c": (qc_s, qc_r, cp), "r": (qr_s, qr_r, right), "l": (ql_s, ql_r, left)}[which]
        slot = zs * 2 + c
        return remote(qx.at[slot, k], qx.at[slot, k], ss.at[zs, k], rs.at[zs, k], dev)

    def q_hop1(k):
        q_own(k).wait()
        q_cross(k).wait_recv()

        @pl.when(has_right)
        def _():
            q_to(z, k, "r").start()

        @pl.when(has_left)
        def _():
            q_to(z, k, "l").start()

        q_to(z, k, "c").start()

    def q_forward(k, d):
        @pl.when(z - d >= 0)
        def _():
            q_to(z - d, k, "r").wait_recv()

            @pl.when(has_right)
            def _():
                q_to(z - d, k, "r").start()

            q_to(z - d, k, "c").start()

        @pl.when(z + d < nz)
        def _():
            q_to(z + d, k, "l").wait_recv()

            @pl.when(has_left)
            def _():
                q_to(z + d, k, "l").start()

            q_to(z + d, k, "c").start()

    def o_core(t, k):
        return (remote(ocs.at[t, k], ocr.at[t, k], oc_s.at[t, k], oc_r.at[t, k], cp),
                remote(mls.at[t, k], mlr.at[t, k], om_s.at[t, k], om_r.at[t, k], cp))

    def o_right(t, k):
        return (remote(r.at[t, k], zlb.at[t, k], zl_s.at[t, k], zl_r.at[t, k], right),
                remote(rml.at[t, k], zlml.at[t, k], zlm_s.at[t, k], zlm_r.at[t, k], right))

    def o_left(t, k):
        return (remote(r.at[t, k], zrb.at[t, k], zr_s.at[t, k], zr_r.at[t, k], left),
                remote(rml.at[t, k], zrml.at[t, k], zrm_s.at[t, k], zrm_r.at[t, k], left))

    def get(o_ref, ml_ref, t, k, h):
        return (o_ref[t, k, h * HDIM:(h + 1) * HDIM, :].astype(F32),
                ml_ref[t, k, h * 8:h * 8 + 1, :], ml_ref[t, k, h * 8 + 1:h * 8 + 2, :])

    def put(o_ref, ml_ref, t, k, h, part):
        o, m, l = part
        o_ref[t, k, h * HDIM:(h + 1) * HDIM, :] = o.astype(BF16)
        row = lax.broadcasted_iota(jnp.int32, (8, both), 0)
        ml_ref[t, k, h * 8:(h + 1) * 8, :] = jnp.where(row == 0, m, l)

    def merge(a, b):
        m = jnp.maximum(a[1], b[1])
        fa, fb_ = jnp.exp2((a[1] - m) * LOG2), jnp.exp2((b[1] - m) * LOG2)
        return a[0] * fa + b[0] * fb_, m, a[2] * fa + b[2] * fb_

    def partial(k, t, cc, h):
        lanes = slice(h * HDIM, (h + 1) * HDIM)
        qs = qx[t * 2 + cc, k, :, :, lanes].reshape(both, HDIM)
        kc = kb[k, :, :, lanes].reshape(both, HDIM)
        mid, lane_half = both // 2 // HDIM * HDIM, both // 2 // HDIM * HDIM + HDIM
        spans = (slice(0, lane_half), slice(mid, both))
        s1 = lax.dot_general(kc, qs, NT, preferred_element_type=F32)
        values, scores = [], []
        for xx in range(2):
            b = t * PLANE + xx * 2 + cc
            picks = [(src, sel[b, src * 4 + slot]) for src in range(2) for slot in range(CAP)]
            kh = jnp.concatenate([hkw[src, n, :, lanes] for src, n in picks], axis=0)
            values.append(jnp.concatenate([hvw[src, n, :, lanes] for src, n in picks], axis=0))
            score = lax.dot_general(kh, qs[spans[xx]], NT, preferred_element_type=F32)
            scores.append(score + bias[t * 2 + cc, xx])

        def joined(op, cur, first, last):
            return jnp.concatenate([
                op(cur[:, :mid], first[:, :mid]),
                op(op(cur[:, mid:lane_half], first[:, mid:]), last[:, :HDIM]),
                op(cur[:, lane_half:], last[:, HDIM:])], axis=1)

        m = joined(jnp.maximum, jnp.max(s1, axis=0, keepdims=True),
                   *[jnp.max(score, axis=0, keepdims=True) for score in scores])
        p1 = jnp.exp2((s1 - m) * LOG2)
        ph = [jnp.exp2((score - m[:, span]) * LOG2) for score, span in zip(scores, spans)]
        cur = jnp.dot(vt[h], p1.astype(BF16), preferred_element_type=F32)
        l = joined(jnp.add, cur[HDIM:HDIM + 1], *[jnp.sum(p, axis=0, keepdims=True) for p in ph])
        o = joined(jnp.add, cur[:HDIM], *[
            lax.dot_general(v, p.astype(BF16), TN, preferred_element_type=F32) for v, p in zip(values, ph)])
        return o, m, l

    def rs_step(k, wave):
        @pl.when((z == wave) & has_right)
        def _():
            def one(i, _):
                t = nz - 1 - i

                @pl.when(t > z)
                def _():
                    @pl.when(has_left)
                    def _():
                        for cpy in o_right(t, k):
                            cpy.wait_recv()
                        for h in range(hc):
                            put(r, rml, t, k, h, merge(get(r, rml, t, k, h), get(zlb, zlml, t, k, h)))
                    for cpy in o_right(t, k):
                        cpy.start()
                return 0
            lax.fori_loop(0, nz, one, 0)

        @pl.when((z == nz - 1 - wave) & has_left)
        def _():
            def one(t, _):
                @pl.when(t < z)
                def _():
                    @pl.when(has_right)
                    def _():
                        for cpy in o_left(t, k):
                            cpy.wait_recv()
                        for h in range(hc):
                            put(r, rml, t, k, h, merge(get(r, rml, t, k, h), get(zrb, zrml, t, k, h)))
                    for cpy in o_left(t, k):
                        cpy.start()
                return 0
            lax.fori_loop(0, nz, one, 0)

    def final_cross(k):
        return remote(fs.at[k], att.at[x, k], f_s.at[k], f_r.at[k], xp)

    def w_fetch(k, side):
        rows = pl.ds(pl.multiple_of(side * half + k * w, HDIM), w)
        return pltpu.make_async_copy(w_in.at[rows], wbuf.at[k % 2, side], w_sem.at[side, k])

    def y_cross(i):
        return remote(ysend.at[i], yrecv.at[i], y_s.at[i], y_r.at[i], yp)

    def project(k):
        final_cross(k).wait_recv()
        for side in range(2):
            w_fetch(k, side).wait()
        a = jnp.concatenate([att[0, k], att[1, k]], axis=1)

        def one(i, _):
            lanes = pl.ds(pl.multiple_of(((1 - hd) * tiles + i) % (2 * tiles) * tile, tile), tile)
            b = wbuf[k % 2, :, :, lanes].reshape(2 * w, tile)
            value = acc[:, lanes] + jnp.dot(a, b, preferred_element_type=F32)
            acc[:, lanes] = value

            @pl.when((k == chunks - 1) & (i < tiles))
            def _():
                ysend[i] = value.astype(BF16)
                y_cross(i).start()
            return 0
        lax.fori_loop(0, 2 * tiles, one, 0)

        @pl.when(k + 2 < chunks)
        def _():
            for side in range(2):
                w_fetch(k + 2, side).start()

    def final(k):
        @pl.when(has_left)
        def _():
            for cpy in o_right(z, k):
                cpy.wait_recv()
            for h in range(hc):
                put(r, rml, z, k, h, merge(get(r, rml, z, k, h), get(zlb, zlml, z, k, h)))

        @pl.when(has_right)
        def _():
            for cpy in o_left(z, k):
                cpy.wait_recv()
            for h in range(hc):
                put(r, rml, z, k, h, merge(get(r, rml, z, k, h), get(zrb, zrml, z, k, h)))

        for h in range(hc):
            o, _, l = get(r, rml, z, k, h)
            done = jnp.transpose(o / l).astype(BF16)
            lanes = slice(h * HDIM, (h + 1) * HDIM)
            mine, theirs = done[:tok], done[tok:]
            att[x, k, :, lanes] = jnp.where(x == 0, mine, theirs)
            fs[k, :, lanes] = jnp.where(x == 0, theirs, mine)
        final_cross(k).start()

    barrier = pltpu.get_barrier_semaphore()
    for dev in (xp, cp, yp):
        pl.semaphore_signal(barrier, inc=1, device_id=dev, device_id_type=MESH)

    @pl.when(has_left)
    def _():
        pl.semaphore_signal(barrier, inc=1, device_id=left, device_id_type=MESH)

    @pl.when(has_right)
    def _():
        pl.semaphore_signal(barrier, inc=1, device_id=right, device_id_type=MESH)

    pl.semaphore_wait(barrier, 3 + has_left.astype(jnp.int32) + has_right.astype(jnp.int32))

    for k in range(chunks):
        q_own(k).start()
    for k in range(min(nz + 1, chunks)):
        q_cross(k).start()
    kv_start(0)
    for k in range(nz + 1, chunks):
        q_cross(k).start()
    if chunks > 1:
        kv_start(1)
    for k in range(min(2, chunks)):
        for side in range(2):
            w_fetch(k, side).start()
    acc[...] = jnp.zeros_like(acc)
    vt[...] = jnp.ones_like(vt)

    mid = both // 2 // HDIM * HDIM
    lane = lax.broadcasted_iota(jnp.int32, (piece, mid + HDIM), 1)

    def fill(i, _):
        t, cc = i // 2, i % 2
        for xx in range(2):
            b = t * PLANE + xx * 2 + cc
            inside = lane >= tok - mid if xx else lane < tok
            for src in range(2):
                for slot in range(CAP):
                    n = src * CAP + slot
                    live = (sel[b, src * 4 + CAP + slot].astype(F32) - 1.0) * 1e30
                    bias[i, xx, n * piece:(n + 1) * piece, :] = jnp.where(inside, live, -1e30)
        return 0

    lax.fori_loop(0, nz * 2, fill, 0)

    for k in range(min(nz + 1, chunks)):
        q_hop1(k)
    for k in range(min(nz - 1, chunks)):
        for d in range(1, nz - k):
            q_forward(k, d)

    def slot_body(j, _):
        k, second = j // 2, j % 2

        @pl.when((k < chunks) & (second == 0))
        def _():
            for i in range(4):
                kv_own(k, i).wait()
                kv_cross(k, i).wait_recv()

            @pl.when(k + 2 < chunks)
            def _():
                kv_start(k + 2)

            @pl.when(k + nz + 1 < chunks)
            def _():
                q_hop1(k + nz + 1)

            for d in range(1, nz):
                @pl.when(k + nz - d < chunks)
                def _():
                    q_forward(k + nz - d, d)
            for h in range(hc):
                vt[h, :HDIM, :] = jnp.transpose(vb[k, :, :, h * HDIM:(h + 1) * HDIM].reshape(both, HDIM))
            hkw[...] = hkb[k].reshape(hkw.shape)
            hvw[...] = hvb[k].reshape(hvw.shape)

            def got(zs, _):
                q_to(zs, k, "c").wait_recv()
                return 0
            lax.fori_loop(0, nz, got, 0)

        @pl.when(k < chunks)
        def _():
            cc = jnp.where(second == 0, 1 - c, c)

            step = 2 if nz % 2 == 0 else 1

            def target(i, _):
                jobs = [(i * step + u, h) for u in range(step) for h in range(hc)]
                parts = [partial(k, t, cc, h) for t, h in jobs]

                @pl.when(second == 0)
                def _():
                    for (t, h), part in zip(jobs, parts):
                        put(ocs, mls, t, k, h, part)
                    for u in range(step):
                        for cpy in o_core(i * step + u, k):
                            cpy.start()

                @pl.when(second == 1)
                def _():
                    for u in range(step):
                        for cpy in o_core(i * step + u, k):
                            cpy.wait_recv()
                    for (t, h), part in zip(jobs, parts):
                        put(r, rml, t, k, h, merge(part, get(ocr, mlr, t, k, h)))
                return 0
            lax.fori_loop(0, nz // step, target, 0)

        def waves(i, _):
            wave = nz - 1 - i
            age = j - 1 - 2 * wave
            kk = age // 2

            @pl.when((age >= 0) & (age % 2 == 0) & (kk < chunks))
            def _():
                rs_step(kk, wave)

                @pl.when(wave == nz - 1)
                def _():
                    final(kk)
            return 0
        lax.fori_loop(0, nz, waves, 0)
        ready = j - 2 * nz

        @pl.when((ready >= 0) & (ready % 2 == 0))
        def _():
            project(ready // 2)
        return 0

    lax.fori_loop(0, 2 * chunks + 2 * nz - 1, slot_body, 0)

    def finish(i, _):
        y_cross(i).wait_recv()
        lanes = pl.ds(pl.multiple_of((hd * tiles + i) * tile, tile), tile)
        out[:, pl.ds(pl.multiple_of(i * tile, tile), tile)] = (acc[:, lanes] + yrecv[i].astype(F32)).astype(BF16)
        y_cross(i).wait_send()
        return 0

    lax.fori_loop(0, tiles, finish, 0)

    def drain(k, _):
        q_cross(k).wait_send()
        for i in range(4):
            kv_cross(k, i).wait_send()
        final_cross(k).wait_send()

        def each(t, _):
            q_to(t, k, "c").wait_send()
            for cpy in o_core(t, k):
                cpy.wait_send()

            @pl.when(has_right & (t <= z))
            def _():
                q_to(t, k, "r").wait_send()

            @pl.when(has_left & (t >= z))
            def _():
                q_to(t, k, "l").wait_send()

            @pl.when(t > z)
            def _():
                for cpy in o_right(t, k):
                    cpy.wait_send()

            @pl.when(t < z)
            def _():
                for cpy in o_left(t, k):
                    cpy.wait_send()
            return 0
        lax.fori_loop(0, nz, each, 0)
        return 0

    lax.fori_loop(0, chunks, drain, 0)


def reader_table(piece_readers, readers):
    hits = jnp.any(piece_readers[:, :, None] == jnp.arange(readers, dtype=jnp.int32)[None, None, :], axis=1)
    hits = hits.astype(jnp.int32)
    rank = jnp.cumsum(hits, axis=0) - hits
    index = jnp.arange(piece_readers.shape[0], dtype=jnp.int32)[:, None]
    where = [jnp.sum(jnp.where((hits > 0) & (rank == n), index, 0), axis=0) for n in range(CAP)]
    count = jnp.sum(hits, axis=0)
    return jnp.stack(where + [(count > n).astype(jnp.int32) for n in range(CAP)], axis=1)


def local_fused(queries, cur_keys, cur_values, hist_keys, hist_values, piece_readers, out_weight):
    tok, width = queries.shape
    hist = hist_keys.shape[0]
    readers = lax.axis_size("seq")
    nz = readers // PLANE
    half_heads = width // HDIM // 2
    hc = 1
    out_width = out_weight.shape[1]
    tile = 512 if out_width % 1024 == 0 else HDIM
    tiles = out_width // 2 // tile
    chunks = half_heads // hc
    w = hc * HDIM
    both = 2 * tok
    piece = hist // piece_readers.shape[0]
    table = reader_table(piece_readers, readers)
    other = lax.ppermute(table, "seq", [(i, i ^ 2) for i in range(readers)])
    sel = jnp.concatenate([table, other], axis=1)
    vm = pltpu.VMEM
    sem = pltpu.SemaphoreType.DMA
    o_buf = vm((nz, chunks, w, both), BF16)
    ml_buf = vm((nz, chunks, hc * 8, both), F32)
    scratch = [
        vm((nz * 2, chunks, 2, tok, w), BF16),
        vm((chunks, 2, tok, w), BF16), vm((chunks, 2, tok, w), BF16),
        vm((chunks, 2, hist, w), BF16), vm((chunks, 2, hist, w), BF16),
        vm((2, hist // piece, piece, w), BF16), vm((2, hist // piece, piece, w), BF16),
        o_buf, ml_buf, o_buf, ml_buf, o_buf, ml_buf, o_buf, ml_buf, o_buf, ml_buf,
        vm((chunks, tok, w), BF16), vm((2, chunks, tok, w), BF16),
        vm((nz * 2, 2, 2 * CAP * piece, both // 2 // HDIM * HDIM + HDIM), F32),
        vm((hc, HDIM + 16, both), BF16),
        vm((2, 2, w, out_width), BF16), vm((tok, out_width), F32),
        vm((tiles, tok, tile), BF16), vm((tiles, tok, tile), BF16),
    ]
    scratch += [sem((chunks,))] * 3 + [sem((4, chunks))] * 3 + [sem((nz, chunks))] * 18
    scratch += [sem((2, chunks))] + [sem((chunks,))] * 2 + [sem((tiles,))] * 2
    any_spec = pl.BlockSpec(memory_space=pl.ANY)
    flops = 4 * readers * tok * (2 * tok + 4 * CAP * piece) * width // 2
    return pl.pallas_call(
        functools.partial(kernel, nz, chunks, hc, piece),
        out_shape=jax.ShapeDtypeStruct((tok, out_width // 2), BF16),
        in_specs=[pl.BlockSpec(memory_space=pltpu.SMEM)] + [any_spec] * 6,
        out_specs=pl.BlockSpec(memory_space=pltpu.VMEM),
        scratch_shapes=scratch,
        compiler_params=pltpu.CompilerParams(
            collective_id=0, has_side_effects=True, vmem_limit_bytes=62 * 1024 * 1024),
        cost_estimate=pl.CostEstimate(flops=flops, bytes_accessed=12 * tok * width, transcendentals=flops // 512),
    )(sel, queries, cur_keys, cur_values, hist_keys, hist_values, out_weight)


def passed_along(value, axis, by):
    length = lax.axis_size(axis)
    return lax.ppermute(value, axis, [(i, (i + by) % length) for i in range(length)])


def attend(totals, query_heads, key_val, valid_keys):
    run_max, run_num, run_sum = totals
    head_count = query_heads.shape[1]
    key_heads = key_val[0].reshape(-1, head_count, HDIM)
    val_heads = key_val[1].reshape(-1, head_count, HDIM)
    scores = jnp.einsum("qhd,khd->hqk", query_heads, key_heads, preferred_element_type=jnp.float32)
    scores = scores * (1.0 / math.sqrt(HDIM))
    if valid_keys is not None:
        scores = jnp.where(valid_keys[None, None, :], scores, -1e30)
    new_max = jnp.maximum(run_max, jnp.max(scores, axis=-1))
    weights = jnp.exp(scores - new_max[..., None])
    if valid_keys is not None:
        weights = jnp.where(valid_keys[None, None, :], weights, 0.0)
    fade_by = jnp.exp(run_max - new_max)
    product = jnp.einsum(
        "hqk,khd->hqd", weights.astype(jnp.bfloat16), val_heads, preferred_element_type=jnp.float32
    )
    run_num = run_num * fade_by[..., None] + product
    run_sum = run_sum * fade_by + jnp.sum(weights, axis=-1)
    return (new_max, run_num, run_sum)


def local(queries, cur_keys, cur_values, hist_keys, hist_values, piece_readers, out_weight):
    tok_rows = queries.shape[0]
    width = queries.shape[1]
    head_count = width // HDIM
    query_heads = queries.reshape(tok_rows, head_count, HDIM)
    reader_count = lax.axis_size("seq")
    owner_rows = piece_readers.shape[0]
    piece_len = hist_keys.shape[0] // owner_rows
    reader_ids = jnp.arange(reader_count, dtype=jnp.int32)
    hits = jnp.sum(
        (piece_readers[:, :, None] == reader_ids[None, None, :]).astype(jnp.int32), axis=1
    )
    earlier = jnp.cumsum(hits, axis=0) - hits
    slot_ids = jnp.arange(CAP, dtype=jnp.int32)
    select = hits[None, :, :] * (earlier[None, :, :] == slot_ids[:, None, None]).astype(jnp.int32)
    select = jnp.transpose(select, (2, 0, 1))
    slot_full = jnp.sum(select, axis=2)[None, :, :]
    stacked = jnp.stack([hist_keys, hist_values]).reshape(2, owner_rows, piece_len * width)
    outgoing = jnp.einsum(
        "rcp,spx->srcx", select.astype(jnp.bfloat16), stacked, preferred_element_type=jnp.float32
    ).astype(jnp.bfloat16)
    arrived, arrived_full = (
        lax.all_to_all(outgoing, "seq", split_axis=1, concat_axis=1, tiled=True),
        lax.all_to_all(slot_full, "seq", split_axis=1, concat_axis=1, tiled=True),
    )
    hist_kv = arrived.reshape(2, -1, width)
    valid_keys = jnp.repeat(arrived_full.reshape(-1), piece_len) > 0
    start_totals = (
        jnp.full((head_count, tok_rows), -1e30, jnp.float32),
        jnp.zeros((head_count, tok_rows, HDIM), jnp.float32),
        jnp.zeros((head_count, tok_rows), jnp.float32),
    )
    totals = attend(start_totals, query_heads, hist_kv, valid_keys)
    own_block = jnp.stack([cur_keys, cur_values])
    totals = attend(totals, query_heads, own_block, None)

    def cycle_turn(step_idx, loop_state):
        travel, inner = loop_state
        travel = passed_along(travel, "seq", 1)
        return (travel, attend(inner, query_heads, travel, None))

    travel_end, totals = lax.fori_loop(0, reader_count - 1, cycle_turn, (own_block, totals))
    run_max, run_num, run_sum = totals
    attended = run_num / run_sum[..., None]
    attended = jnp.transpose(attended, (1, 0, 2)).reshape(tok_rows, width).astype(jnp.bfloat16)
    partial_out = jnp.dot(attended, out_weight, preferred_element_type=jnp.float32)
    return lax.psum_scatter(
        partial_out.astype(jnp.bfloat16), "head", scatter_dimension=1, tiled=True
    )


def solution(mesh):
    placed = (
        P("seq", "head"),
        P("seq", "head"),
        P("seq", "head"),
        P("seq", "head"),
        P("seq", "head"),
        P("seq", None),
        P("head", None),
    )

    def run(*args):
        heads = args[0].shape[1] // mesh.shape["head"] // HDIM
        whole_planes = mesh.shape["seq"] % PLANE == 0 and heads % 2 == 0 and mesh.shape["head"] == 2
        whole_planes = whole_planes and args[0].shape[0] // mesh.shape["seq"] % HDIM == HDIM // 2
        return jax.shard_map(
            local_fused if whole_planes else local,
            mesh=mesh, in_specs=placed, out_specs=P("seq", "head"), check_vma=False,
        )(*args)

    return run
```

```python
import functools
import math

import jax
import jax.numpy as jnp
from jax import lax
from jax.experimental import pallas as pl
from jax.experimental.pallas import tpu as pltpu
from jax.sharding import PartitionSpec as P

HDIM = 128
CAP = 2
PLANE = 4
LOG2 = math.log2(math.e) / math.sqrt(HDIM)
MESH = pl.DeviceIdType.MESH
F32 = jnp.float32
BF16 = jnp.bfloat16
NT = (((1,), (1,)), ((), ()))
TN = (((0,), (0,)), ((), ()))


def kernel(nz, chunks, hc, piece, sel, q_in, k_in, v_in, hk_in, hv_in, w_in, out,
           qx, kb, vb, hkb, hvb, hkw, hvw, ocs, mls, ocr, mlr, r, rml, zlb, zlml, zrb, zrml, fs, att, bias, vt,
           wbuf, acc, ysend, yrecv, wy, atty,
           q_loc, q_xs, q_xr, kv_loc, kv_xs, kv_xr,
           qc_s, qc_r, qr_s, qr_r, ql_s, ql_r,
           oc_s, oc_r, om_s, om_r, zl_s, zl_r, zlm_s, zlm_r, zr_s, zr_r, zrm_s, zrm_r,
           w_sem, f_s, f_r, y_s, y_r, wy_s, wy_r, ay_s, ay_r):
    s = lax.axis_index("seq")
    hd = lax.axis_index("head")
    z, x, c = s // PLANE, (s // 2) % 2, s % 2
    tok = q_in.shape[0]
    both = 2 * tok
    w = hc * HDIM
    half = chunks * w
    xp = (z * PLANE + (1 - x) * 2 + c, hd)
    cp = (z * PLANE + x * 2 + (1 - c), hd)
    left = (jnp.maximum(s - PLANE, 0), hd)
    right = (jnp.minimum(s + PLANE, nz * PLANE - 1), hd)
    yp = (s, 1 - hd)
    tiles, _, tile = ysend.shape
    late = wy.shape[0]
    early = chunks - late
    has_left, has_right = z > 0, z < nz - 1
    own = z * 2 + c

    def remote(src, dst, ss, rs, dev):
        return pltpu.make_async_remote_copy(
            src_ref=src, dst_ref=dst, send_sem=ss, recv_sem=rs, device_id=dev, device_id_type=MESH)

    def cols(side, k):
        return pl.ds(pl.multiple_of(side * half + k * w, HDIM), w)

    def q_own(k):
        return pltpu.make_async_copy(q_in.at[:, cols(x, k)], qx.at[own, k, x], q_loc.at[k])

    def q_cross(k):
        return remote(q_in.at[:, cols(1 - x, k)], qx.at[own, k, x], q_xs.at[k], q_xr.at[k], xp)

    pairs = ((k_in, kb), (v_in, vb), (hk_in, hkb), (hv_in, hvb))

    def kv_own(k, i):
        return pltpu.make_async_copy(pairs[i][0].at[:, cols(x, k)], pairs[i][1].at[k, 0], kv_loc.at[i, k])

    def kv_cross(k, i):
        return remote(pairs[i][0].at[:, cols(1 - x, k)], pairs[i][1].at[k, 1], kv_xs.at[i, k], kv_xr.at[i, k], xp)

    def kv_start(k):
        for i in range(4):
            kv_own(k, i).start()
            kv_cross(k, i).start()

    def q_to(zs, k, which):
        ss, rs, dev = {"c": (qc_s, qc_r, cp), "r": (qr_s, qr_r, right), "l": (ql_s, ql_r, left)}[which]
        slot = zs * 2 + c
        return remote(qx.at[slot, k], qx.at[slot, k], ss.at[zs, k], rs.at[zs, k], dev)

    def q_hop1(k):
        q_own(k).wait()
        q_cross(k).wait_recv()

        @pl.when(has_right)
        def _():
            q_to(z, k, "r").start()

        @pl.when(has_left)
        def _():
            q_to(z, k, "l").start()

        q_to(z, k, "c").start()

    def q_forward(k, d):
        @pl.when(z - d >= 0)
        def _():
            q_to(z - d, k, "r").wait_recv()

            @pl.when(has_right)
            def _():
                q_to(z - d, k, "r").start()

            q_to(z - d, k, "c").start()

        @pl.when(z + d < nz)
        def _():
            q_to(z + d, k, "l").wait_recv()

            @pl.when(has_left)
            def _():
                q_to(z + d, k, "l").start()

            q_to(z + d, k, "c").start()

    def o_core(t, k):
        return (remote(ocs.at[t, k], ocr.at[t, k], oc_s.at[t, k], oc_r.at[t, k], cp),
                remote(mls.at[t, k], mlr.at[t, k], om_s.at[t, k], om_r.at[t, k], cp))

    def o_right(t, k):
        return (remote(r.at[t, k], zlb.at[t, k], zl_s.at[t, k], zl_r.at[t, k], right),
                remote(rml.at[t, k], zlml.at[t, k], zlm_s.at[t, k], zlm_r.at[t, k], right))

    def o_left(t, k):
        return (remote(r.at[t, k], zrb.at[t, k], zr_s.at[t, k], zr_r.at[t, k], left),
                remote(rml.at[t, k], zrml.at[t, k], zrm_s.at[t, k], zrm_r.at[t, k], left))

    def get(o_ref, ml_ref, t, k, h):
        return (o_ref[t, k, h * HDIM:(h + 1) * HDIM, :].astype(F32),
                ml_ref[t, k, h * 8:h * 8 + 1, :], ml_ref[t, k, h * 8 + 1:h * 8 + 2, :])

    def put(o_ref, ml_ref, t, k, h, part):
        o, m, l = part
        o_ref[t, k, h * HDIM:(h + 1) * HDIM, :] = o.astype(BF16)
        row = lax.broadcasted_iota(jnp.int32, (8, both), 0)
        ml_ref[t, k, h * 8:(h + 1) * 8, :] = jnp.where(row == 0, m, l)

    def merge(a, b):
        m = jnp.maximum(a[1], b[1])
        fa, fb_ = jnp.exp2((a[1] - m) * LOG2), jnp.exp2((b[1] - m) * LOG2)
        return a[0] * fa + b[0] * fb_, m, a[2] * fa + b[2] * fb_

    def partial(k, t, cc, h):
        lanes = slice(h * HDIM, (h + 1) * HDIM)
        qs = qx[t * 2 + cc, k, :, :, lanes].reshape(both, HDIM)
        kc = kb[k, :, :, lanes].reshape(both, HDIM)
        mid, lane_half = both // 2 // HDIM * HDIM, both // 2 // HDIM * HDIM + HDIM
        spans = (slice(0, lane_half), slice(mid, both))
        s1 = lax.dot_general(kc, qs, NT, preferred_element_type=F32)
        values, scores = [], []
        for xx in range(2):
            b = t * PLANE + xx * 2 + cc
            picks = [(src, sel[b, src * 4 + slot]) for src in range(2) for slot in range(CAP)]
            kh = jnp.concatenate([hkw[src, n, :, lanes] for src, n in picks], axis=0)
            values.append(jnp.concatenate([hvw[src, n, :, lanes] for src, n in picks], axis=0))
            score = lax.dot_general(kh, qs[spans[xx]], NT, preferred_element_type=F32)
            scores.append(score + bias[t * 2 + cc, xx])

        def joined(op, cur, first, last):
            return jnp.concatenate([
                op(cur[:, :mid], first[:, :mid]),
                op(op(cur[:, mid:lane_half], first[:, mid:]), last[:, :HDIM]),
                op(cur[:, lane_half:], last[:, HDIM:])], axis=1)

        m = joined(jnp.maximum, jnp.max(s1, axis=0, keepdims=True),
                   *[jnp.max(score, axis=0, keepdims=True) for score in scores])
        p1 = jnp.exp2((s1 - m) * LOG2)
        ph = [jnp.exp2((score - m[:, span]) * LOG2) for score, span in zip(scores, spans)]
        cur = jnp.dot(vt[h], p1.astype(BF16), preferred_element_type=F32)
        l = joined(jnp.add, cur[HDIM:HDIM + 1], *[jnp.sum(p, axis=0, keepdims=True) for p in ph])
        o = joined(jnp.add, cur[:HDIM], *[
            lax.dot_general(v, p.astype(BF16), TN, preferred_element_type=F32) for v, p in zip(values, ph)])
        return o, m, l

    def rs_step(k, wave):
        @pl.when((z == wave) & has_right)
        def _():
            def one(i, _):
                t = nz - 1 - i

                @pl.when(t > z)
                def _():
                    @pl.when(has_left)
                    def _():
                        for cpy in o_right(t, k):
                            cpy.wait_recv()
                        for h in range(hc):
                            put(r, rml, t, k, h, merge(get(r, rml, t, k, h), get(zlb, zlml, t, k, h)))
                    for cpy in o_right(t, k):
                        cpy.start()
                return 0
            lax.fori_loop(0, nz, one, 0)

        @pl.when((z == nz - 1 - wave) & has_left)
        def _():
            def one(t, _):
                @pl.when(t < z)
                def _():
                    @pl.when(has_right)
                    def _():
                        for cpy in o_left(t, k):
                            cpy.wait_recv()
                        for h in range(hc):
                            put(r, rml, t, k, h, merge(get(r, rml, t, k, h), get(zrb, zrml, t, k, h)))
                    for cpy in o_left(t, k):
                        cpy.start()
                return 0
            lax.fori_loop(0, nz, one, 0)

    def final_cross(k):
        return remote(fs.at[k], att.at[x, k], f_s.at[k], f_r.at[k], xp)

    def w_fetch(k, side):
        rows = pl.ds(pl.multiple_of(side * half + k * w, HDIM), w)
        return pltpu.make_async_copy(w_in.at[rows], wbuf.at[k % 2, side], w_sem.at[side, k])

    def y_cross(i):
        return remote(ysend.at[i], yrecv.at[i], y_s.at[i], y_r.at[i], yp)

    def wy_cross(g, side):
        rows = pl.ds(pl.multiple_of(side * half + (early + g) * w, HDIM), w)
        lanes = pl.ds(pl.multiple_of((1 - hd) * tiles * tile, tile), tiles * tile)
        return remote(w_in.at[rows, lanes], wy.at[g, side], wy_s.at[g, side], wy_r.at[g, side], yp)

    def atty_cross(g):
        return remote(att.at[:, early + g], atty.at[g], ay_s.at[g], ay_r.at[g], yp)

    def project(k):
        final_cross(k).wait_recv()

        @pl.when(k >= early)
        def _():
            atty_cross(k - early).start()

        for side in range(2):
            w_fetch(k, side).wait()
        a = jnp.concatenate([att[0, k], att[1, k]], axis=1)

        def one(i, _):
            lanes = pl.ds(pl.multiple_of(((1 - hd) * tiles + i) % (2 * tiles) * tile, tile), tile)
            b = wbuf[k % 2, :, :, lanes].reshape(2 * w, tile)
            value = acc[:, lanes] + jnp.dot(a, b, preferred_element_type=F32)
            acc[:, lanes] = value

            @pl.when((k == early - 1) & (i < tiles))
            def _():
                ysend[i] = value.astype(BF16)
                y_cross(i).start()
            return 0
        lax.fori_loop(jnp.where(k < early, 0, tiles), 2 * tiles, one, 0)

        @pl.when(k + 2 < chunks)
        def _():
            for side in range(2):
                w_fetch(k + 2, side).start()

        @pl.when(k >= early)
        def _():
            g = k - early
            for side in range(2):
                wy_cross(g, side).wait_recv()
            atty_cross(g).wait_recv()
            a = jnp.concatenate([atty[g, 0], atty[g, 1]], axis=1)

            def one(i, _):
                lanes = pl.ds(pl.multiple_of((hd * tiles + i) * tile, tile), tile)
                b = wy[g, :, :, pl.ds(pl.multiple_of(i * tile, tile), tile)].reshape(2 * w, tile)
                acc[:, lanes] += jnp.dot(a, b, preferred_element_type=F32)
                return 0
            lax.fori_loop(0, tiles, one, 0)

    def final(k):
        @pl.when(has_left)
        def _():
            for cpy in o_right(z, k):
                cpy.wait_recv()
            for h in range(hc):
                put(r, rml, z, k, h, merge(get(r, rml, z, k, h), get(zlb, zlml, z, k, h)))

        @pl.when(has_right)
        def _():
            for cpy in o_left(z, k):
                cpy.wait_recv()
            for h in range(hc):
                put(r, rml, z, k, h, merge(get(r, rml, z, k, h), get(zrb, zrml, z, k, h)))

        for h in range(hc):
            o, _, l = get(r, rml, z, k, h)
            done = jnp.transpose(o / l).astype(BF16)
            lanes = slice(h * HDIM, (h + 1) * HDIM)
            mine, theirs = done[:tok], done[tok:]
            att[x, k, :, lanes] = jnp.where(x == 0, mine, theirs)
            fs[k, :, lanes] = jnp.where(x == 0, theirs, mine)
        final_cross(k).start()

    barrier = pltpu.get_barrier_semaphore()
    for dev in (xp, cp, yp):
        pl.semaphore_signal(barrier, inc=1, device_id=dev, device_id_type=MESH)

    @pl.when(has_left)
    def _():
        pl.semaphore_signal(barrier, inc=1, device_id=left, device_id_type=MESH)

    @pl.when(has_right)
    def _():
        pl.semaphore_signal(barrier, inc=1, device_id=right, device_id_type=MESH)

    pl.semaphore_wait(barrier, 3 + has_left.astype(jnp.int32) + has_right.astype(jnp.int32))

    for k in range(chunks):
        q_own(k).start()
    for k in range(min(nz + 1, chunks)):
        q_cross(k).start()
    kv_start(0)
    for k in range(nz + 1, chunks):
        q_cross(k).start()
    if chunks > 1:
        kv_start(1)
    for g in range(late):
        for side in range(2):
            wy_cross(g, side).start()
    for k in range(min(2, chunks)):
        for side in range(2):
            w_fetch(k, side).start()
    acc[...] = jnp.zeros_like(acc)
    vt[...] = jnp.ones_like(vt)

    mid = both // 2 // HDIM * HDIM
    lane = lax.broadcasted_iota(jnp.int32, (piece, mid + HDIM), 1)

    def fill(i, _):
        t, cc = i // 2, i % 2
        for xx in range(2):
            b = t * PLANE + xx * 2 + cc
            inside = lane >= tok - mid if xx else lane < tok
            for src in range(2):
                for slot in range(CAP):
                    n = src * CAP + slot
                    live = (sel[b, src * 4 + CAP + slot].astype(F32) - 1.0) * 1e30
                    bias[i, xx, n * piece:(n + 1) * piece, :] = jnp.where(inside, live, -1e30)
        return 0

    lax.fori_loop(0, nz * 2, fill, 0)

    ahead = [2 * (nz - d) - 1 for d in range(nz)]
    ahead[0] = 2 * nz
    for k in range(min(nz + 1, chunks)):
        q_hop1(k)
    for d in range(1, nz):
        q_forward(0, d)
    for k in range(min(nz + 1, chunks), min(ahead[0], chunks)):
        q_hop1(k)
    for k in range(1, chunks):
        for d in range(1, nz):
            if k < ahead[d]:
                q_forward(k, d)

    def slot_body(j, _):
        k, second = j // 2, j % 2

        @pl.when((k < chunks) & (second == 0))
        def _():
            for i in range(4):
                kv_own(k, i).wait()
                kv_cross(k, i).wait_recv()

            @pl.when(k + 2 < chunks)
            def _():
                kv_start(k + 2)

            @pl.when(k + ahead[0] < chunks)
            def _():
                q_hop1(k + ahead[0])

            for d in range(1, nz):
                @pl.when(k + ahead[d] < chunks)
                def _():
                    q_forward(k + ahead[d], d)
            for h in range(hc):
                vt[h, :HDIM, :] = jnp.transpose(vb[k, :, :, h * HDIM:(h + 1) * HDIM].reshape(both, HDIM))
            hkw[...] = hkb[k].reshape(hkw.shape)
            hvw[...] = hvb[k].reshape(hvw.shape)

            def got(zs, _):
                q_to(zs, k, "c").wait_recv()
                return 0
            lax.fori_loop(0, nz, got, 0)

        @pl.when(k < chunks)
        def _():
            cc = jnp.where(second == 0, 1 - c, c)

            step = 2 if nz % 2 == 0 else 1

            def target(i, _):
                jobs = [(i * step + u, h) for u in range(step) for h in range(hc)]
                parts = [partial(k, t, cc, h) for t, h in jobs]

                @pl.when(second == 0)
                def _():
                    for (t, h), part in zip(jobs, parts):
                        put(ocs, mls, t, k, h, part)
                    for u in range(step):
                        for cpy in o_core(i * step + u, k):
                            cpy.start()

                @pl.when(second == 1)
                def _():
                    for u in range(step):
                        for cpy in o_core(i * step + u, k):
                            cpy.wait_recv()
                    for (t, h), part in zip(jobs, parts):
                        put(r, rml, t, k, h, merge(part, get(ocr, mlr, t, k, h)))
                return 0
            lax.fori_loop(0, nz // step, target, 0)

        def waves(i, _):
            wave = nz - 1 - i
            age = j - 1 - 2 * wave
            kk = age // 2

            @pl.when((age >= 0) & (age % 2 == 0) & (kk < chunks))
            def _():
                rs_step(kk, wave)

                @pl.when(wave == nz - 1)
                def _():
                    final(kk)
            return 0
        lax.fori_loop(0, nz, waves, 0)
        ready = j - 2 * nz

        @pl.when((ready >= 0) & (ready % 2 == 0))
        def _():
            project(ready // 2)
        return 0

    lax.fori_loop(0, 2 * chunks + 2 * nz - 1, slot_body, 0)

    def finish(i, _):
        y_cross(i).wait_recv()
        lanes = pl.ds(pl.multiple_of((hd * tiles + i) * tile, tile), tile)
        out[:, pl.ds(pl.multiple_of(i * tile, tile), tile)] = (acc[:, lanes] + yrecv[i].astype(F32)).astype(BF16)
        y_cross(i).wait_send()
        return 0

    lax.fori_loop(0, tiles, finish, 0)
    for g in range(late):
        atty_cross(g).wait_send()
        for side in range(2):
            wy_cross(g, side).wait_send()

    def drain(k, _):
        q_cross(k).wait_send()
        for i in range(4):
            kv_cross(k, i).wait_send()
        final_cross(k).wait_send()

        def each(t, _):
            q_to(t, k, "c").wait_send()
            for cpy in o_core(t, k):
                cpy.wait_send()

            @pl.when(has_right & (t <= z))
            def _():
                q_to(t, k, "r").wait_send()

            @pl.when(has_left & (t >= z))
            def _():
                q_to(t, k, "l").wait_send()

            @pl.when(t > z)
            def _():
                for cpy in o_right(t, k):
                    cpy.wait_send()

            @pl.when(t < z)
            def _():
                for cpy in o_left(t, k):
                    cpy.wait_send()
            return 0
        lax.fori_loop(0, nz, each, 0)
        return 0

    lax.fori_loop(0, chunks, drain, 0)


def reader_table(piece_readers, readers):
    hits = jnp.any(piece_readers[:, :, None] == jnp.arange(readers, dtype=jnp.int32)[None, None, :], axis=1)
    hits = hits.astype(jnp.int32)
    rank = jnp.cumsum(hits, axis=0) - hits
    index = jnp.arange(piece_readers.shape[0], dtype=jnp.int32)[:, None]
    where = [jnp.sum(jnp.where((hits > 0) & (rank == n), index, 0), axis=0) for n in range(CAP)]
    count = jnp.sum(hits, axis=0)
    return jnp.stack(where + [(count > n).astype(jnp.int32) for n in range(CAP)], axis=1)


def local_fused(queries, cur_keys, cur_values, hist_keys, hist_values, piece_readers, out_weight):
    tok, width = queries.shape
    hist = hist_keys.shape[0]
    readers = lax.axis_size("seq")
    nz = readers // PLANE
    half_heads = width // HDIM // 2
    hc = 1
    out_width = out_weight.shape[1]
    tile = 512 if out_width % 1024 == 0 else HDIM
    tiles = out_width // 2 // tile
    late = 2
    chunks = half_heads // hc
    w = hc * HDIM
    both = 2 * tok
    piece = hist // piece_readers.shape[0]
    table = reader_table(piece_readers, readers)
    other = lax.ppermute(table, "seq", [(i, i ^ 2) for i in range(readers)])
    sel = jnp.concatenate([table, other], axis=1)
    vm = pltpu.VMEM
    sem = pltpu.SemaphoreType.DMA
    o_buf = vm((nz, chunks, w, both), BF16)
    ml_buf = vm((nz, chunks, hc * 8, both), F32)
    scratch = [
        vm((nz * 2, chunks, 2, tok, w), BF16),
        vm((chunks, 2, tok, w), BF16), vm((chunks, 2, tok, w), BF16),
        vm((chunks, 2, hist, w), BF16), vm((chunks, 2, hist, w), BF16),
        vm((2, hist // piece, piece, w), BF16), vm((2, hist // piece, piece, w), BF16),
        o_buf, ml_buf, o_buf, ml_buf, o_buf, ml_buf, o_buf, ml_buf, o_buf, ml_buf,
        vm((chunks, tok, w), BF16), vm((2, chunks, tok, w), BF16),
        vm((nz * 2, 2, 2 * CAP * piece, both // 2 // HDIM * HDIM + HDIM), F32),
        vm((hc, HDIM + 16, both), BF16),
        vm((2, 2, w, out_width), BF16), vm((tok, out_width), F32),
        vm((tiles, tok, tile), BF16), vm((tiles, tok, tile), BF16),
        vm((late, 2, w, out_width // 2), BF16), vm((late, 2, tok, w), BF16),
    ]
    scratch += [sem((chunks,))] * 3 + [sem((4, chunks))] * 3 + [sem((nz, chunks))] * 18
    scratch += [sem((2, chunks))] + [sem((chunks,))] * 2 + [sem((tiles,))] * 2
    scratch += [sem((late, 2))] * 2 + [sem((late,))] * 2
    any_spec = pl.BlockSpec(memory_space=pl.ANY)
    flops = 4 * readers * tok * (2 * tok + 4 * CAP * piece) * width // 2
    return pl.pallas_call(
        functools.partial(kernel, nz, chunks, hc, piece),
        out_shape=jax.ShapeDtypeStruct((tok, out_width // 2), BF16),
        in_specs=[pl.BlockSpec(memory_space=pltpu.SMEM)] + [any_spec] * 6,
        out_specs=pl.BlockSpec(memory_space=pltpu.VMEM),
        scratch_shapes=scratch,
        compiler_params=pltpu.CompilerParams(
            collective_id=0, has_side_effects=True, vmem_limit_bytes=62 * 1024 * 1024),
        cost_estimate=pl.CostEstimate(flops=flops, bytes_accessed=12 * tok * width, transcendentals=flops // 512),
    )(sel, queries, cur_keys, cur_values, hist_keys, hist_values, out_weight)


def passed_along(value, axis, by):
    length = lax.axis_size(axis)
    return lax.ppermute(value, axis, [(i, (i + by) % length) for i in range(length)])


def attend(totals, query_heads, key_val, valid_keys):
    run_max, run_num, run_sum = totals
    head_count = query_heads.shape[1]
    key_heads = key_val[0].reshape(-1, head_count, HDIM)
    val_heads = key_val[1].reshape(-1, head_count, HDIM)
    scores = jnp.einsum("qhd,khd->hqk", query_heads, key_heads, preferred_element_type=jnp.float32)
    scores = scores * (1.0 / math.sqrt(HDIM))
    if valid_keys is not None:
        scores = jnp.where(valid_keys[None, None, :], scores, -1e30)
    new_max = jnp.maximum(run_max, jnp.max(scores, axis=-1))
    weights = jnp.exp(scores - new_max[..., None])
    if valid_keys is not None:
        weights = jnp.where(valid_keys[None, None, :], weights, 0.0)
    fade_by = jnp.exp(run_max - new_max)
    product = jnp.einsum(
        "hqk,khd->hqd", weights.astype(jnp.bfloat16), val_heads, preferred_element_type=jnp.float32
    )
    run_num = run_num * fade_by[..., None] + product
    run_sum = run_sum * fade_by + jnp.sum(weights, axis=-1)
    return (new_max, run_num, run_sum)


def local(queries, cur_keys, cur_values, hist_keys, hist_values, piece_readers, out_weight):
    tok_rows = queries.shape[0]
    width = queries.shape[1]
    head_count = width // HDIM
    query_heads = queries.reshape(tok_rows, head_count, HDIM)
    reader_count = lax.axis_size("seq")
    owner_rows = piece_readers.shape[0]
    piece_len = hist_keys.shape[0] // owner_rows
    reader_ids = jnp.arange(reader_count, dtype=jnp.int32)
    hits = jnp.sum(
        (piece_readers[:, :, None] == reader_ids[None, None, :]).astype(jnp.int32), axis=1
    )
    earlier = jnp.cumsum(hits, axis=0) - hits
    slot_ids = jnp.arange(CAP, dtype=jnp.int32)
    select = hits[None, :, :] * (earlier[None, :, :] == slot_ids[:, None, None]).astype(jnp.int32)
    select = jnp.transpose(select, (2, 0, 1))
    slot_full = jnp.sum(select, axis=2)[None, :, :]
    stacked = jnp.stack([hist_keys, hist_values]).reshape(2, owner_rows, piece_len * width)
    outgoing = jnp.einsum(
        "rcp,spx->srcx", select.astype(jnp.bfloat16), stacked, preferred_element_type=jnp.float32
    ).astype(jnp.bfloat16)
    arrived, arrived_full = (
        lax.all_to_all(outgoing, "seq", split_axis=1, concat_axis=1, tiled=True),
        lax.all_to_all(slot_full, "seq", split_axis=1, concat_axis=1, tiled=True),
    )
    hist_kv = arrived.reshape(2, -1, width)
    valid_keys = jnp.repeat(arrived_full.reshape(-1), piece_len) > 0
    start_totals = (
        jnp.full((head_count, tok_rows), -1e30, jnp.float32),
        jnp.zeros((head_count, tok_rows, HDIM), jnp.float32),
        jnp.zeros((head_count, tok_rows), jnp.float32),
    )
    totals = attend(start_totals, query_heads, hist_kv, valid_keys)
    own_block = jnp.stack([cur_keys, cur_values])
    totals = attend(totals, query_heads, own_block, None)

    def cycle_turn(step_idx, loop_state):
        travel, inner = loop_state
        travel = passed_along(travel, "seq", 1)
        return (travel, attend(inner, query_heads, travel, None))

    travel_end, totals = lax.fori_loop(0, reader_count - 1, cycle_turn, (own_block, totals))
    run_max, run_num, run_sum = totals
    attended = run_num / run_sum[..., None]
    attended = jnp.transpose(attended, (1, 0, 2)).reshape(tok_rows, width).astype(jnp.bfloat16)
    partial_out = jnp.dot(attended, out_weight, preferred_element_type=jnp.float32)
    return lax.psum_scatter(
        partial_out.astype(jnp.bfloat16), "head", scatter_dimension=1, tiled=True
    )


def solution(mesh):
    placed = (
        P("seq", "head"),
        P("seq", "head"),
        P("seq", "head"),
        P("seq", "head"),
        P("seq", "head"),
        P("seq", None),
        P("head", None),
    )

    def run(*args):
        heads = args[0].shape[1] // mesh.shape["head"] // HDIM
        whole_planes = mesh.shape["seq"] % PLANE == 0 and heads % 2 == 0 and heads > 4 and mesh.shape["head"] == 2
        whole_planes = whole_planes and args[0].shape[0] // mesh.shape["seq"] % HDIM == HDIM // 2
        return jax.shard_map(
            local_fused if whole_planes else local,
            mesh=mesh, in_specs=placed, out_specs=P("seq", "head"), check_vma=False,
        )(*args)

    return run
```

```python
import functools
import math

import jax
import jax.numpy as jnp
from jax import lax
from jax.experimental import pallas as pl
from jax.experimental.pallas import tpu as pltpu
from jax.sharding import PartitionSpec as P

HDIM = 128
CAP = 2
PLANE = 4
LOG2 = math.log2(math.e) / math.sqrt(HDIM)
MESH = pl.DeviceIdType.MESH
F32 = jnp.float32
BF16 = jnp.bfloat16
NT = (((1,), (1,)), ((), ()))
TN = (((0,), (0,)), ((), ()))


def kernel(nz, chunks, hc, piece, tab_in, q_in, k_in, v_in, hk_in, hv_in, w_in, out,
           qx, kb, vb, hkb, hvb, hkw, hvw, ocs, mls, ocr, mlr, r, rml, zlb, zlml, zrb, zrml, fs, att, bias, vt,
           wbuf, acc, ysend, yrecv, wy, atty,
           q_loc, q_xs, q_xr, kv_loc, kv_xs, kv_xr,
           qc_s, qc_r, qr_s, qr_r, ql_s, ql_r,
           oc_s, oc_r, om_s, om_r, zl_s, zl_r, zlm_s, zlm_r, zr_s, zr_r, zrm_s, zrm_r,
           w_sem, f_s, f_r, y_s, y_r, wy_s, wy_r, ay_s, ay_r,
           sel, tab, tab_l, tab_s, tab_r):
    s = lax.axis_index("seq")
    hd = lax.axis_index("head")
    z, x, c = s // PLANE, (s // 2) % 2, s % 2
    tok = q_in.shape[0]
    both = 2 * tok
    w = hc * HDIM
    half = chunks * w
    xp = (z * PLANE + (1 - x) * 2 + c, hd)
    cp = (z * PLANE + x * 2 + (1 - c), hd)
    left = (jnp.maximum(s - PLANE, 0), hd)
    right = (jnp.minimum(s + PLANE, nz * PLANE - 1), hd)
    yp = (s, 1 - hd)
    tiles, _, tile = ysend.shape
    late = wy.shape[0]
    early = chunks - late
    parts = 4
    pieces = late * 2 * parts
    has_left, has_right = z > 0, z < nz - 1
    own = z * 2 + c

    def remote(src, dst, ss, rs, dev):
        return pltpu.make_async_remote_copy(
            src_ref=src, dst_ref=dst, send_sem=ss, recv_sem=rs, device_id=dev, device_id_type=MESH)

    def cols(side, k):
        return pl.ds(pl.multiple_of(side * half + k * w, HDIM), w)

    def q_own(k):
        return pltpu.make_async_copy(q_in.at[:, cols(x, k)], qx.at[own, k, x], q_loc.at[k])

    def q_cross(k):
        return remote(q_in.at[:, cols(1 - x, k)], qx.at[own, k, x], q_xs.at[k], q_xr.at[k], xp)

    pairs = ((k_in, kb), (v_in, vb), (hk_in, hkb), (hv_in, hvb))

    def kv_own(k, i):
        return pltpu.make_async_copy(pairs[i][0].at[:, cols(x, k)], pairs[i][1].at[k, 0], kv_loc.at[i, k])

    def kv_cross(k, i):
        return remote(pairs[i][0].at[:, cols(1 - x, k)], pairs[i][1].at[k, 1], kv_xs.at[i, k], kv_xr.at[i, k], xp)

    def kv_start(k):
        for i in range(4):
            kv_own(k, i).start()
            kv_cross(k, i).start()

    def q_to(zs, k, which):
        ss, rs, dev = {"c": (qc_s, qc_r, cp), "r": (qr_s, qr_r, right), "l": (ql_s, ql_r, left)}[which]
        slot = zs * 2 + c
        return remote(qx.at[slot, k], qx.at[slot, k], ss.at[zs, k], rs.at[zs, k], dev)

    def q_hop1(k):
        q_own(k).wait()
        q_cross(k).wait_recv()

        @pl.when(has_right)
        def _():
            q_to(z, k, "r").start()

        @pl.when(has_left)
        def _():
            q_to(z, k, "l").start()

        q_to(z, k, "c").start()

    def q_forward(k, d):
        @pl.when(z - d >= 0)
        def _():
            q_to(z - d, k, "r").wait_recv()

            @pl.when(has_right)
            def _():
                q_to(z - d, k, "r").start()

            q_to(z - d, k, "c").start()

        @pl.when(z + d < nz)
        def _():
            q_to(z + d, k, "l").wait_recv()

            @pl.when(has_left)
            def _():
                q_to(z + d, k, "l").start()

            q_to(z + d, k, "c").start()

    def o_core(t, k):
        return (remote(ocs.at[t, k], ocr.at[t, k], oc_s.at[t, k], oc_r.at[t, k], cp),
                remote(mls.at[t, k], mlr.at[t, k], om_s.at[t, k], om_r.at[t, k], cp))

    def o_right(t, k):
        return (remote(r.at[t, k], zlb.at[t, k], zl_s.at[t, k], zl_r.at[t, k], right),
                remote(rml.at[t, k], zlml.at[t, k], zlm_s.at[t, k], zlm_r.at[t, k], right))

    def o_left(t, k):
        return (remote(r.at[t, k], zrb.at[t, k], zr_s.at[t, k], zr_r.at[t, k], left),
                remote(rml.at[t, k], zrml.at[t, k], zrm_s.at[t, k], zrm_r.at[t, k], left))

    def get(o_ref, ml_ref, t, k, h):
        return (o_ref[t, k, h * HDIM:(h + 1) * HDIM, :].astype(F32),
                ml_ref[t, k, h * 8:h * 8 + 1, :], ml_ref[t, k, h * 8 + 1:h * 8 + 2, :])

    def put(o_ref, ml_ref, t, k, h, part):
        o, m, l = part
        o_ref[t, k, h * HDIM:(h + 1) * HDIM, :] = o.astype(BF16)
        row = lax.broadcasted_iota(jnp.int32, (8, both), 0)
        ml_ref[t, k, h * 8:(h + 1) * 8, :] = jnp.where(row == 0, m, l)

    def merge(a, b):
        m = jnp.maximum(a[1], b[1])
        fa, fb_ = jnp.exp2((a[1] - m) * LOG2), jnp.exp2((b[1] - m) * LOG2)
        return a[0] * fa + b[0] * fb_, m, a[2] * fa + b[2] * fb_

    def partial(k, t, cc, h):
        lanes = slice(h * HDIM, (h + 1) * HDIM)
        qs = qx[t * 2 + cc, k, :, :, lanes].reshape(both, HDIM)
        kc = kb[k, :, :, lanes].reshape(both, HDIM)
        mid, lane_half = both // 2 // HDIM * HDIM, both // 2 // HDIM * HDIM + HDIM
        spans = (slice(0, lane_half), slice(mid, both))
        s1 = lax.dot_general(kc, qs, NT, preferred_element_type=F32)
        values, scores = [], []
        for xx in range(2):
            b = t * PLANE + xx * 2 + cc
            picks = [(src, sel[src, b, slot]) for src in range(2) for slot in range(CAP)]
            kh = jnp.concatenate([hkw[src, n, :, lanes] for src, n in picks], axis=0)
            values.append(jnp.concatenate([hvw[src, n, :, lanes] for src, n in picks], axis=0))
            score = lax.dot_general(kh, qs[spans[xx]], NT, preferred_element_type=F32)
            scores.append(score + bias[t * 2 + cc, xx])

        def joined(op, cur, first, last):
            return jnp.concatenate([
                op(cur[:, :mid], first[:, :mid]),
                op(op(cur[:, mid:lane_half], first[:, mid:]), last[:, :HDIM]),
                op(cur[:, lane_half:], last[:, HDIM:])], axis=1)

        m = joined(jnp.maximum, jnp.max(s1, axis=0, keepdims=True),
                   *[jnp.max(score, axis=0, keepdims=True) for score in scores])
        p1 = jnp.exp2((s1 - m) * LOG2)
        ph = [jnp.exp2((score - m[:, span]) * LOG2) for score, span in zip(scores, spans)]
        cur = jnp.dot(vt[h], p1.astype(BF16), preferred_element_type=F32)
        l = joined(jnp.add, cur[HDIM:HDIM + 1], *[jnp.sum(p, axis=0, keepdims=True) for p in ph])
        o = joined(jnp.add, cur[:HDIM], *[
            lax.dot_general(v, p.astype(BF16), TN, preferred_element_type=F32) for v, p in zip(values, ph)])
        return o, m, l

    def rs_step(k, wave):
        @pl.when((z == wave) & has_right)
        def _():
            def one(i, _):
                t = nz - 1 - i

                @pl.when(t > z)
                def _():
                    @pl.when(has_left)
                    def _():
                        for cpy in o_right(t, k):
                            cpy.wait_recv()
                        for h in range(hc):
                            put(r, rml, t, k, h, merge(get(r, rml, t, k, h), get(zlb, zlml, t, k, h)))
                    for cpy in o_right(t, k):
                        cpy.start()
                return 0
            lax.fori_loop(0, nz, one, 0)

        @pl.when((z == nz - 1 - wave) & has_left)
        def _():
            def one(t, _):
                @pl.when(t < z)
                def _():
                    @pl.when(has_right)
                    def _():
                        for cpy in o_left(t, k):
                            cpy.wait_recv()
                        for h in range(hc):
                            put(r, rml, t, k, h, merge(get(r, rml, t, k, h), get(zrb, zrml, t, k, h)))
                    for cpy in o_left(t, k):
                        cpy.start()
                return 0
            lax.fori_loop(0, nz, one, 0)

    def final_cross(k):
        return remote(fs.at[k], att.at[x, k], f_s.at[k], f_r.at[k], xp)

    def w_fetch(k, side):
        rows = pl.ds(pl.multiple_of(side * half + k * w, HDIM), w)
        return pltpu.make_async_copy(w_in.at[rows], wbuf.at[k % 2, side], w_sem.at[side, k])

    def y_cross(i):
        return remote(ysend.at[i], yrecv.at[i], y_s.at[i], y_r.at[i], yp)

    def wy_cross(n):
        g, side, part = n // (2 * parts), n // parts % 2, n % parts
        rows = pl.ds(pl.multiple_of(side * half + (early + g) * w + part * (w // parts), w // parts), w // parts)
        lanes = pl.ds(pl.multiple_of((1 - hd) * tiles * tile, tile), tiles * tile)
        into = wy.at[g, side, pl.ds(pl.multiple_of(part * (w // parts), w // parts), w // parts)]
        return remote(w_in.at[rows, lanes], into, wy_s.at[n], wy_r.at[n], yp)

    def atty_cross(g):
        return remote(att.at[:, early + g], atty.at[g], ay_s.at[g], ay_r.at[g], yp)

    def project(k):
        final_cross(k).wait_recv()

        @pl.when(k >= early)
        def _():
            atty_cross(k - early).start()

        for side in range(2):
            w_fetch(k, side).wait()
        a = jnp.concatenate([att[0, k], att[1, k]], axis=1)

        def one(i, _):
            lanes = pl.ds(pl.multiple_of(((1 - hd) * tiles + i) % (2 * tiles) * tile, tile), tile)
            b = wbuf[k % 2, :, :, lanes].reshape(2 * w, tile)
            value = acc[:, lanes] + jnp.dot(a, b, preferred_element_type=F32)
            acc[:, lanes] = value

            @pl.when((k == early - 1) & (i < tiles))
            def _():
                ysend[i] = value.astype(BF16)
                y_cross(i).start()
            return 0
        lax.fori_loop(jnp.where(k < early, 0, tiles), 2 * tiles, one, 0)

        @pl.when(k + 2 < chunks)
        def _():
            for side in range(2):
                w_fetch(k + 2, side).start()

        @pl.when(k >= early)
        def _():
            g = k - early
            for n in range(2 * parts):
                wy_cross(g * 2 * parts + n).wait_recv()
            atty_cross(g).wait_recv()
            a = jnp.concatenate([atty[g, 0], atty[g, 1]], axis=1)

            def one(i, _):
                lanes = pl.ds(pl.multiple_of((hd * tiles + i) * tile, tile), tile)
                b = wy[g, :, :, pl.ds(pl.multiple_of(i * tile, tile), tile)].reshape(2 * w, tile)
                acc[:, lanes] += jnp.dot(a, b, preferred_element_type=F32)
                return 0
            lax.fori_loop(0, tiles, one, 0)

    def final(k):
        @pl.when(has_left)
        def _():
            for cpy in o_right(z, k):
                cpy.wait_recv()
            for h in range(hc):
                put(r, rml, z, k, h, merge(get(r, rml, z, k, h), get(zlb, zlml, z, k, h)))

        @pl.when(has_right)
        def _():
            for cpy in o_left(z, k):
                cpy.wait_recv()
            for h in range(hc):
                put(r, rml, z, k, h, merge(get(r, rml, z, k, h), get(zrb, zrml, z, k, h)))

        for h in range(hc):
            o, _, l = get(r, rml, z, k, h)
            done = jnp.transpose(o / l).astype(BF16)
            lanes = slice(h * HDIM, (h + 1) * HDIM)
            mine, theirs = done[:tok], done[tok:]
            att[x, k, :, lanes] = jnp.where(x == 0, mine, theirs)
            fs[k, :, lanes] = jnp.where(x == 0, theirs, mine)
        final_cross(k).start()

    barrier = pltpu.get_barrier_semaphore()
    for dev in (xp, cp, yp):
        pl.semaphore_signal(barrier, inc=1, device_id=dev, device_id_type=MESH)

    @pl.when(has_left)
    def _():
        pl.semaphore_signal(barrier, inc=1, device_id=left, device_id_type=MESH)

    @pl.when(has_right)
    def _():
        pl.semaphore_signal(barrier, inc=1, device_id=right, device_id_type=MESH)

    pl.semaphore_wait(barrier, 3 + has_left.astype(jnp.int32) + has_right.astype(jnp.int32))

    tab_cross = remote(tab_in, tab, tab_s.at[0], tab_r.at[0], xp)
    tab_cross.start()
    tab_own = pltpu.make_async_copy(tab_in, sel.at[0], tab_l.at[0])
    tab_own.start()
    for k in range(chunks):
        q_own(k).start()
    for k in range(min(nz + 1, chunks)):
        q_cross(k).start()
    kv_start(0)
    for k in range(nz + 1, chunks):
        q_cross(k).start()
    if chunks > 1:
        kv_start(1)
    for k in range(min(2, chunks)):
        for side in range(2):
            w_fetch(k, side).start()
    acc[...] = jnp.zeros_like(acc)
    vt[...] = jnp.ones_like(vt)

    mid = both // 2 // HDIM * HDIM
    lane = lax.broadcasted_iota(jnp.int32, (piece, mid + HDIM), 1)

    def fill(i, _):
        t, cc = i // 2, i % 2
        for xx in range(2):
            b = t * PLANE + xx * 2 + cc
            inside = lane >= tok - mid if xx else lane < tok
            for src in range(2):
                for slot in range(CAP):
                    n = src * CAP + slot
                    live = (sel[src, b, CAP + slot].astype(F32) - 1.0) * 1e30
                    bias[i, xx, n * piece:(n + 1) * piece, :] = jnp.where(inside, live, -1e30)
        return 0

    tab_own.wait()
    tab_cross.wait()
    tab_other = pltpu.make_async_copy(tab, sel.at[1], tab_l.at[1])
    tab_other.start()
    tab_other.wait()
    lax.fori_loop(0, nz * 2, fill, 0)

    for k in range(min(nz + 1, chunks)):
        q_hop1(k)
    for k in range(min(nz - 1, chunks)):
        for d in range(1, nz - k):
            q_forward(k, d)

    def slot_body(j, _):
        k, second = j // 2, j % 2

        @pl.when((j >= 1) & (j <= pieces))
        def _():
            wy_cross(j - 1).start()

        @pl.when((k < chunks) & (second == 0))
        def _():
            for i in range(4):
                kv_own(k, i).wait()
                kv_cross(k, i).wait_recv()

            @pl.when(k + 2 < chunks)
            def _():
                kv_start(k + 2)

            @pl.when(k + nz + 1 < chunks)
            def _():
                q_hop1(k + nz + 1)

            for d in range(1, nz):
                @pl.when(k + nz - d < chunks)
                def _():
                    q_forward(k + nz - d, d)
            for h in range(hc):
                vt[h, :HDIM, :] = jnp.transpose(vb[k, :, :, h * HDIM:(h + 1) * HDIM].reshape(both, HDIM))
            hkw[...] = hkb[k].reshape(hkw.shape)
            hvw[...] = hvb[k].reshape(hvw.shape)

            def got(zs, _):
                q_to(zs, k, "c").wait_recv()
                return 0
            lax.fori_loop(0, nz, got, 0)

        @pl.when(k < chunks)
        def _():
            cc = jnp.where(second == 0, 1 - c, c)

            step = 2 if nz % 2 == 0 else 1

            def target(i, _):
                jobs = [(i * step + u, h) for u in range(step) for h in range(hc)]
                parts = [partial(k, t, cc, h) for t, h in jobs]

                @pl.when(second == 0)
                def _():
                    for (t, h), part in zip(jobs, parts):
                        put(ocs, mls, t, k, h, part)
                    for u in range(step):
                        for cpy in o_core(i * step + u, k):
                            cpy.start()

                @pl.when(second == 1)
                def _():
                    for u in range(step):
                        for cpy in o_core(i * step + u, k):
                            cpy.wait_recv()
                    for (t, h), part in zip(jobs, parts):
                        put(r, rml, t, k, h, merge(part, get(ocr, mlr, t, k, h)))
                return 0
            lax.fori_loop(0, nz // step, target, 0)

        def waves(i, _):
            wave = nz - 1 - i
            age = j - 1 - 2 * wave
            kk = age // 2

            @pl.when((age >= 0) & (age % 2 == 0) & (kk < chunks))
            def _():
                rs_step(kk, wave)

                @pl.when(wave == nz - 1)
                def _():
                    final(kk)
            return 0
        lax.fori_loop(0, nz, waves, 0)
        ready = j - 2 * nz

        @pl.when((ready >= 0) & (ready % 2 == 0))
        def _():
            project(ready // 2)
        return 0

    lax.fori_loop(0, 2 * chunks + 2 * nz - 1, slot_body, 0)

    def finish(i, _):
        y_cross(i).wait_recv()
        lanes = pl.ds(pl.multiple_of((hd * tiles + i) * tile, tile), tile)
        out[:, pl.ds(pl.multiple_of(i * tile, tile), tile)] = (acc[:, lanes] + yrecv[i].astype(F32)).astype(BF16)
        y_cross(i).wait_send()
        return 0

    lax.fori_loop(0, tiles, finish, 0)
    for g in range(late):
        atty_cross(g).wait_send()
    for n in range(pieces):
        wy_cross(n).wait_send()

    def drain(k, _):
        q_cross(k).wait_send()
        for i in range(4):
            kv_cross(k, i).wait_send()
        final_cross(k).wait_send()

        def each(t, _):
            q_to(t, k, "c").wait_send()
            for cpy in o_core(t, k):
                cpy.wait_send()

            @pl.when(has_right & (t <= z))
            def _():
                q_to(t, k, "r").wait_send()

            @pl.when(has_left & (t >= z))
            def _():
                q_to(t, k, "l").wait_send()

            @pl.when(t > z)
            def _():
                for cpy in o_right(t, k):
                    cpy.wait_send()

            @pl.when(t < z)
            def _():
                for cpy in o_left(t, k):
                    cpy.wait_send()
            return 0
        lax.fori_loop(0, nz, each, 0)
        return 0

    lax.fori_loop(0, chunks, drain, 0)


def reader_table(piece_readers, readers):
    hits = jnp.any(piece_readers[:, :, None] == jnp.arange(readers, dtype=jnp.int32)[None, None, :], axis=1)
    hits = hits.astype(jnp.int32)
    rank = jnp.cumsum(hits, axis=0) - hits
    index = jnp.arange(piece_readers.shape[0], dtype=jnp.int32)[:, None]
    where = [jnp.sum(jnp.where((hits > 0) & (rank == n), index, 0), axis=0) for n in range(CAP)]
    count = jnp.sum(hits, axis=0)
    return jnp.stack(where + [(count > n).astype(jnp.int32) for n in range(CAP)], axis=1)


def local_fused(queries, cur_keys, cur_values, hist_keys, hist_values, piece_readers, out_weight):
    tok, width = queries.shape
    hist = hist_keys.shape[0]
    readers = lax.axis_size("seq")
    nz = readers // PLANE
    half_heads = width // HDIM // 2
    hc = 1
    out_width = out_weight.shape[1]
    tile = 512 if out_width % 1024 == 0 else HDIM
    tiles = out_width // 2 // tile
    late = 2
    chunks = half_heads // hc
    w = hc * HDIM
    both = 2 * tok
    piece = hist // piece_readers.shape[0]
    table = reader_table(piece_readers, readers)
    table = jnp.pad(table, ((0, 0), (0, HDIM - table.shape[1])))
    vm = pltpu.VMEM
    sem = pltpu.SemaphoreType.DMA
    o_buf = vm((nz, chunks, w, both), BF16)
    ml_buf = vm((nz, chunks, hc * 8, both), F32)
    scratch = [
        vm((nz * 2, chunks, 2, tok, w), BF16),
        vm((chunks, 2, tok, w), BF16), vm((chunks, 2, tok, w), BF16),
        vm((chunks, 2, hist, w), BF16), vm((chunks, 2, hist, w), BF16),
        vm((2, hist // piece, piece, w), BF16), vm((2, hist // piece, piece, w), BF16),
        o_buf, ml_buf, o_buf, ml_buf, o_buf, ml_buf, o_buf, ml_buf, o_buf, ml_buf,
        vm((chunks, tok, w), BF16), vm((2, chunks, tok, w), BF16),
        vm((nz * 2, 2, 2 * CAP * piece, both // 2 // HDIM * HDIM + HDIM), F32),
        vm((hc, HDIM + 16, both), BF16),
        vm((2, 2, w, out_width), BF16), vm((tok, out_width), F32),
        vm((tiles, tok, tile), BF16), vm((tiles, tok, tile), BF16),
        vm((late, 2, w, out_width // 2), BF16), vm((late, 2, tok, w), BF16),
    ]
    scratch += [sem((chunks,))] * 3 + [sem((4, chunks))] * 3 + [sem((nz, chunks))] * 18
    scratch += [sem((2, chunks))] + [sem((chunks,))] * 2 + [sem((tiles,))] * 2
    scratch += [sem((late * 8,))] * 2 + [sem((late,))] * 2
    scratch += [pltpu.SMEM((2, readers, HDIM), jnp.int32), vm((readers, HDIM), jnp.int32), sem((2,)), sem((1,)), sem((1,))]
    any_spec = pl.BlockSpec(memory_space=pl.ANY)
    flops = 4 * readers * tok * (2 * tok + 4 * CAP * piece) * width // 2
    return pl.pallas_call(
        functools.partial(kernel, nz, chunks, hc, piece),
        out_shape=jax.ShapeDtypeStruct((tok, out_width // 2), BF16),
        in_specs=[any_spec] * 7,
        out_specs=pl.BlockSpec(memory_space=pltpu.VMEM),
        scratch_shapes=scratch,
        compiler_params=pltpu.CompilerParams(
            collective_id=0, has_side_effects=True, vmem_limit_bytes=62 * 1024 * 1024),
        cost_estimate=pl.CostEstimate(flops=flops, bytes_accessed=12 * tok * width, transcendentals=flops // 512),
    )(table, queries, cur_keys, cur_values, hist_keys, hist_values, out_weight)


def passed_along(value, axis, by):
    length = lax.axis_size(axis)
    return lax.ppermute(value, axis, [(i, (i + by) % length) for i in range(length)])


def attend(totals, query_heads, key_val, valid_keys):
    run_max, run_num, run_sum = totals
    head_count = query_heads.shape[1]
    key_heads = key_val[0].reshape(-1, head_count, HDIM)
    val_heads = key_val[1].reshape(-1, head_count, HDIM)
    scores = jnp.einsum("qhd,khd->hqk", query_heads, key_heads, preferred_element_type=jnp.float32)
    scores = scores * (1.0 / math.sqrt(HDIM))
    if valid_keys is not None:
        scores = jnp.where(valid_keys[None, None, :], scores, -1e30)
    new_max = jnp.maximum(run_max, jnp.max(scores, axis=-1))
    weights = jnp.exp(scores - new_max[..., None])
    if valid_keys is not None:
        weights = jnp.where(valid_keys[None, None, :], weights, 0.0)
    fade_by = jnp.exp(run_max - new_max)
    product = jnp.einsum(
        "hqk,khd->hqd", weights.astype(jnp.bfloat16), val_heads, preferred_element_type=jnp.float32
    )
    run_num = run_num * fade_by[..., None] + product
    run_sum = run_sum * fade_by + jnp.sum(weights, axis=-1)
    return (new_max, run_num, run_sum)


def local(queries, cur_keys, cur_values, hist_keys, hist_values, piece_readers, out_weight):
    tok_rows = queries.shape[0]
    width = queries.shape[1]
    head_count = width // HDIM
    query_heads = queries.reshape(tok_rows, head_count, HDIM)
    reader_count = lax.axis_size("seq")
    owner_rows = piece_readers.shape[0]
    piece_len = hist_keys.shape[0] // owner_rows
    reader_ids = jnp.arange(reader_count, dtype=jnp.int32)
    hits = jnp.sum(
        (piece_readers[:, :, None] == reader_ids[None, None, :]).astype(jnp.int32), axis=1
    )
    earlier = jnp.cumsum(hits, axis=0) - hits
    slot_ids = jnp.arange(CAP, dtype=jnp.int32)
    select = hits[None, :, :] * (earlier[None, :, :] == slot_ids[:, None, None]).astype(jnp.int32)
    select = jnp.transpose(select, (2, 0, 1))
    slot_full = jnp.sum(select, axis=2)[None, :, :]
    stacked = jnp.stack([hist_keys, hist_values]).reshape(2, owner_rows, piece_len * width)
    outgoing = jnp.einsum(
        "rcp,spx->srcx", select.astype(jnp.bfloat16), stacked, preferred_element_type=jnp.float32
    ).astype(jnp.bfloat16)
    arrived, arrived_full = (
        lax.all_to_all(outgoing, "seq", split_axis=1, concat_axis=1, tiled=True),
        lax.all_to_all(slot_full, "seq", split_axis=1, concat_axis=1, tiled=True),
    )
    hist_kv = arrived.reshape(2, -1, width)
    valid_keys = jnp.repeat(arrived_full.reshape(-1), piece_len) > 0
    start_totals = (
        jnp.full((head_count, tok_rows), -1e30, jnp.float32),
        jnp.zeros((head_count, tok_rows, HDIM), jnp.float32),
        jnp.zeros((head_count, tok_rows), jnp.float32),
    )
    totals = attend(start_totals, query_heads, hist_kv, valid_keys)
    own_block = jnp.stack([cur_keys, cur_values])
    totals = attend(totals, query_heads, own_block, None)

    def cycle_turn(step_idx, loop_state):
        travel, inner = loop_state
        travel = passed_along(travel, "seq", 1)
        return (travel, attend(inner, query_heads, travel, None))

    travel_end, totals = lax.fori_loop(0, reader_count - 1, cycle_turn, (own_block, totals))
    run_max, run_num, run_sum = totals
    attended = run_num / run_sum[..., None]
    attended = jnp.transpose(attended, (1, 0, 2)).reshape(tok_rows, width).astype(jnp.bfloat16)
    partial_out = jnp.dot(attended, out_weight, preferred_element_type=jnp.float32)
    return lax.psum_scatter(
        partial_out.astype(jnp.bfloat16), "head", scatter_dimension=1, tiled=True
    )


def solution(mesh):
    placed = (
        P("seq", "head"),
        P("seq", "head"),
        P("seq", "head"),
        P("seq", "head"),
        P("seq", "head"),
        P("seq", None),
        P("head", None),
    )

    def run(*args):
        heads = args[0].shape[1] // mesh.shape["head"] // HDIM
        whole_planes = mesh.shape["seq"] % PLANE == 0 and heads % 2 == 0 and heads > 4 and mesh.shape["head"] == 2
        whole_planes = whole_planes and args[0].shape[0] // mesh.shape["seq"] % HDIM == HDIM // 2
        return jax.shard_map(
            local_fused if whole_planes else local,
            mesh=mesh, in_specs=placed, out_specs=P("seq", "head"), check_vma=False,
        )(*args)

    return run
```

```python
import functools
import math

import jax
import jax.numpy as jnp
from jax import lax
from jax.experimental import pallas as pl
from jax.experimental.pallas import tpu as pltpu
from jax.sharding import PartitionSpec as P

HDIM = 128
CAP = 2
PLANE = 4
LOG2 = math.log2(math.e) / math.sqrt(HDIM)
MESH = pl.DeviceIdType.MESH
F32 = jnp.float32
BF16 = jnp.bfloat16
NT = (((1,), (1,)), ((), ()))
TN = (((0,), (0,)), ((), ()))


def kernel(nz, chunks, hc, piece, tab_in, q_in, k_in, v_in, hk_in, hv_in, w_in, out,
           qx, kb, vb, hkb, hvb, hkw, hvw, ocs, mls, ocr, mlr, r, rml, zlb, zlml, zrb, zrml, fs, att, bias, vt,
           wbuf, acc, ysend, yrecv, wy, atty,
           q_loc, q_xs, q_xr, kv_loc, kv_xs, kv_xr,
           qc_s, qc_r, qr_s, qr_r, ql_s, ql_r,
           oc_s, oc_r, om_s, om_r, zl_s, zl_r, zlm_s, zlm_r, zr_s, zr_r, zrm_s, zrm_r,
           w_sem, f_s, f_r, y_s, y_r, wy_s, wy_r, ay_s, ay_r,
           sel, tab, tab_l, tab_s, tab_r):
    s = lax.axis_index("seq")
    hd = lax.axis_index("head")
    z, x, c = s // PLANE, (s // 2) % 2, s % 2
    tok = q_in.shape[0]
    both = 2 * tok
    w = hc * HDIM
    half = chunks * w
    xp = (z * PLANE + (1 - x) * 2 + c, hd)
    cp = (z * PLANE + x * 2 + (1 - c), hd)
    left = (jnp.maximum(s - PLANE, 0), hd)
    right = (jnp.minimum(s + PLANE, nz * PLANE - 1), hd)
    yp = (s, 1 - hd)
    tiles, _, tile = ysend.shape
    late = wy.shape[0]
    early = chunks - late
    parts = 4
    pieces = late * 2 * parts
    has_left, has_right = z > 0, z < nz - 1
    own = z * 2 + c

    def remote(src, dst, ss, rs, dev):
        return pltpu.make_async_remote_copy(
            src_ref=src, dst_ref=dst, send_sem=ss, recv_sem=rs, device_id=dev, device_id_type=MESH)

    def cols(side, k):
        return pl.ds(pl.multiple_of(side * half + k * w, HDIM), w)

    def q_own(k):
        return pltpu.make_async_copy(q_in.at[:, cols(x, k)], qx.at[own, k, x], q_loc.at[k])

    def q_cross(k):
        return remote(q_in.at[:, cols(1 - x, k)], qx.at[own, k, x], q_xs.at[k], q_xr.at[k], xp)

    pairs = ((k_in, kb), (v_in, vb), (hk_in, hkb), (hv_in, hvb))

    def kv_own(k, i):
        return pltpu.make_async_copy(pairs[i][0].at[:, cols(x, k)], pairs[i][1].at[k, 0], kv_loc.at[i, k])

    def kv_cross(k, i):
        return remote(pairs[i][0].at[:, cols(1 - x, k)], pairs[i][1].at[k, 1], kv_xs.at[i, k], kv_xr.at[i, k], xp)

    def kv_start(k):
        for i in range(4):
            kv_own(k, i).start()
            kv_cross(k, i).start()

    def q_to(zs, k, which):
        ss, rs, dev = {"c": (qc_s, qc_r, cp), "r": (qr_s, qr_r, right), "l": (ql_s, ql_r, left)}[which]
        slot = zs * 2 + c
        return remote(qx.at[slot, k], qx.at[slot, k], ss.at[zs, k], rs.at[zs, k], dev)

    def q_hop1(k):
        q_own(k).wait()
        q_cross(k).wait_recv()

        @pl.when(has_right)
        def _():
            q_to(z, k, "r").start()

        @pl.when(has_left)
        def _():
            q_to(z, k, "l").start()

        q_to(z, k, "c").start()

    def q_forward(k, d):
        @pl.when(z - d >= 0)
        def _():
            q_to(z - d, k, "r").wait_recv()

            @pl.when(has_right)
            def _():
                q_to(z - d, k, "r").start()

            q_to(z - d, k, "c").start()

        @pl.when(z + d < nz)
        def _():
            q_to(z + d, k, "l").wait_recv()

            @pl.when(has_left)
            def _():
                q_to(z + d, k, "l").start()

            q_to(z + d, k, "c").start()

    def o_core(t, k):
        return (remote(ocs.at[t, k], ocr.at[t, k], oc_s.at[t, k], oc_r.at[t, k], cp),
                remote(mls.at[t, k], mlr.at[t, k], om_s.at[t, k], om_r.at[t, k], cp))

    def o_right(t, k):
        return (remote(r.at[t, k], zlb.at[t, k], zl_s.at[t, k], zl_r.at[t, k], right),
                remote(rml.at[t, k], zlml.at[t, k], zlm_s.at[t, k], zlm_r.at[t, k], right))

    def o_left(t, k):
        return (remote(r.at[t, k], zrb.at[t, k], zr_s.at[t, k], zr_r.at[t, k], left),
                remote(rml.at[t, k], zrml.at[t, k], zrm_s.at[t, k], zrm_r.at[t, k], left))

    def get(o_ref, ml_ref, t, k, h):
        return (o_ref[t, k, h * HDIM:(h + 1) * HDIM, :].astype(F32),
                ml_ref[t, k, h * 8:h * 8 + 1, :], ml_ref[t, k, h * 8 + 1:h * 8 + 2, :])

    def put(o_ref, ml_ref, t, k, h, part):
        o, m, l = part
        o_ref[t, k, h * HDIM:(h + 1) * HDIM, :] = o.astype(BF16)
        row = lax.broadcasted_iota(jnp.int32, (8, both), 0)
        ml_ref[t, k, h * 8:(h + 1) * 8, :] = jnp.where(row == 0, m, l)

    def merge(a, b):
        m = jnp.maximum(a[1], b[1])
        fa, fb_ = jnp.exp2((a[1] - m) * LOG2), jnp.exp2((b[1] - m) * LOG2)
        return a[0] * fa + b[0] * fb_, m, a[2] * fa + b[2] * fb_

    def partial(k, t, cc, h):
        lanes = slice(h * HDIM, (h + 1) * HDIM)
        qs = qx[t * 2 + cc, k, :, :, lanes].reshape(both, HDIM)
        kc = kb[k, :, :, lanes].reshape(both, HDIM)
        mid, lane_half = both // 2 // HDIM * HDIM, both // 2 // HDIM * HDIM + HDIM
        spans = (slice(0, lane_half), slice(mid, both))
        s1 = lax.dot_general(kc, qs, NT, preferred_element_type=F32)
        values, scores = [], []
        for xx in range(2):
            b = t * PLANE + xx * 2 + cc
            picks = [(src, sel[src, b, slot]) for src in range(2) for slot in range(CAP)]
            kh = jnp.concatenate([hkw[src, n, :, lanes] for src, n in picks], axis=0)
            values.append(jnp.concatenate([hvw[src, n, :, lanes] for src, n in picks], axis=0))
            score = lax.dot_general(kh, qs[spans[xx]], NT, preferred_element_type=F32)
            scores.append(score + bias[t * 2 + cc, xx])

        def joined(op, cur, first, last):
            return jnp.concatenate([
                op(cur[:, :mid], first[:, :mid]),
                op(op(cur[:, mid:lane_half], first[:, mid:]), last[:, :HDIM]),
                op(cur[:, lane_half:], last[:, HDIM:])], axis=1)

        m = joined(jnp.maximum, jnp.max(s1, axis=0, keepdims=True),
                   *[jnp.max(score, axis=0, keepdims=True) for score in scores])
        p1 = jnp.exp2((s1 - m) * LOG2)
        ph = [jnp.exp2((score - m[:, span]) * LOG2) for score, span in zip(scores, spans)]
        cur = jnp.dot(vt[h], p1.astype(BF16), preferred_element_type=F32)
        l = joined(jnp.add, cur[HDIM:HDIM + 1], *[jnp.sum(p, axis=0, keepdims=True) for p in ph])
        o = joined(jnp.add, cur[:HDIM], *[
            lax.dot_general(v, p.astype(BF16), TN, preferred_element_type=F32) for v, p in zip(values, ph)])
        return o, m, l

    def rs_step(k, wave):
        @pl.when((z == wave) & has_right)
        def _():
            def one(i, _):
                t = nz - 1 - i

                @pl.when(t > z)
                def _():
                    @pl.when(has_left)
                    def _():
                        for cpy in o_right(t, k):
                            cpy.wait_recv()
                        for h in range(hc):
                            put(r, rml, t, k, h, merge(get(r, rml, t, k, h), get(zlb, zlml, t, k, h)))
                    for cpy in o_right(t, k):
                        cpy.start()
                return 0
            lax.fori_loop(0, nz, one, 0)

        @pl.when((z == nz - 1 - wave) & has_left)
        def _():
            def one(t, _):
                @pl.when(t < z)
                def _():
                    @pl.when(has_right)
                    def _():
                        for cpy in o_left(t, k):
                            cpy.wait_recv()
                        for h in range(hc):
                            put(r, rml, t, k, h, merge(get(r, rml, t, k, h), get(zrb, zrml, t, k, h)))
                    for cpy in o_left(t, k):
                        cpy.start()
                return 0
            lax.fori_loop(0, nz, one, 0)

    def final_cross(k):
        return remote(fs.at[k], att.at[x, k], f_s.at[k], f_r.at[k], xp)

    def w_fetch(k, side):
        rows = pl.ds(pl.multiple_of(side * half + k * w, HDIM), w)
        return pltpu.make_async_copy(w_in.at[rows], wbuf.at[k % 2, side], w_sem.at[side, k])

    def y_cross(i):
        return remote(ysend.at[i], yrecv.at[i], y_s.at[i], y_r.at[i], yp)

    def wy_cross(n):
        g, side, part = n // (2 * parts), n // parts % 2, n % parts
        rows = pl.ds(pl.multiple_of(side * half + (early + g) * w + part * (w // parts), w // parts), w // parts)
        lanes = pl.ds(pl.multiple_of((1 - hd) * tiles * tile, tile), tiles * tile)
        into = wy.at[g, side, pl.ds(pl.multiple_of(part * (w // parts), w // parts), w // parts)]
        return remote(w_in.at[rows, lanes], into, wy_s.at[n], wy_r.at[n], yp)

    def atty_cross(g):
        return remote(att.at[:, early + g], atty.at[g], ay_s.at[g], ay_r.at[g], yp)

    def project(k):
        final_cross(k).wait_recv()

        @pl.when(k >= early)
        def _():
            atty_cross(k - early).start()

        for side in range(2):
            w_fetch(k, side).wait()
        a = jnp.concatenate([att[0, k], att[1, k]], axis=1)

        def one(i, _):
            lanes = pl.ds(pl.multiple_of(((1 - hd) * tiles + i) % (2 * tiles) * tile, tile), tile)
            b = wbuf[k % 2, :, :, lanes].reshape(2 * w, tile)
            value = acc[:, lanes] + jnp.dot(a, b, preferred_element_type=F32)
            acc[:, lanes] = value

            @pl.when((k == early - 1) & (i < tiles))
            def _():
                ysend[i] = value.astype(BF16)
                y_cross(i).start()
            return 0
        lax.fori_loop(jnp.where(k < early, 0, tiles), 2 * tiles, one, 0)

        @pl.when(k + 2 < chunks)
        def _():
            for side in range(2):
                w_fetch(k + 2, side).start()

        @pl.when(k >= early)
        def _():
            g = k - early
            for n in range(2 * parts):
                wy_cross(g * 2 * parts + n).wait_recv()
            atty_cross(g).wait_recv()
            a = jnp.concatenate([atty[g, 0], atty[g, 1]], axis=1)

            def one(i, _):
                lanes = pl.ds(pl.multiple_of((hd * tiles + i) * tile, tile), tile)
                b = wy[g, :, :, pl.ds(pl.multiple_of(i * tile, tile), tile)].reshape(2 * w, tile)
                acc[:, lanes] += jnp.dot(a, b, preferred_element_type=F32)
                return 0
            lax.fori_loop(0, tiles, one, 0)

    def final(k):
        @pl.when(has_left)
        def _():
            for cpy in o_right(z, k):
                cpy.wait_recv()
            for h in range(hc):
                put(r, rml, z, k, h, merge(get(r, rml, z, k, h), get(zlb, zlml, z, k, h)))

        @pl.when(has_right)
        def _():
            for cpy in o_left(z, k):
                cpy.wait_recv()
            for h in range(hc):
                put(r, rml, z, k, h, merge(get(r, rml, z, k, h), get(zrb, zrml, z, k, h)))

        for h in range(hc):
            o, _, l = get(r, rml, z, k, h)
            done = jnp.transpose(o / l).astype(BF16)
            lanes = slice(h * HDIM, (h + 1) * HDIM)
            mine, theirs = done[:tok], done[tok:]
            att[x, k, :, lanes] = jnp.where(x == 0, mine, theirs)
            fs[k, :, lanes] = jnp.where(x == 0, theirs, mine)
        final_cross(k).start()

    barrier = pltpu.get_barrier_semaphore()
    for dev in (xp, cp, yp):
        pl.semaphore_signal(barrier, inc=1, device_id=dev, device_id_type=MESH)

    @pl.when(has_left)
    def _():
        pl.semaphore_signal(barrier, inc=1, device_id=left, device_id_type=MESH)

    @pl.when(has_right)
    def _():
        pl.semaphore_signal(barrier, inc=1, device_id=right, device_id_type=MESH)

    pl.semaphore_wait(barrier, 3 + has_left.astype(jnp.int32) + has_right.astype(jnp.int32))

    tab_cross = remote(tab_in, tab, tab_s.at[0], tab_r.at[0], xp)
    tab_cross.start()
    tab_own = pltpu.make_async_copy(tab_in, sel.at[0], tab_l.at[0])
    tab_own.start()
    for k in range(chunks):
        q_own(k).start()
    for k in range(min(nz + 1, chunks)):
        q_cross(k).start()
    kv_start(0)
    for k in range(nz + 1, chunks):
        q_cross(k).start()
    if chunks > 1:
        kv_start(1)
    for k in range(min(2, chunks)):
        for side in range(2):
            w_fetch(k, side).start()
    acc[...] = jnp.zeros_like(acc)
    vt[...] = jnp.ones_like(vt)

    mid = both // 2 // HDIM * HDIM
    lane = lax.broadcasted_iota(jnp.int32, (piece, mid + HDIM), 1)

    def fill(i, _):
        t, cc = i // 2, i % 2
        for xx in range(2):
            b = t * PLANE + xx * 2 + cc
            inside = lane >= tok - mid if xx else lane < tok
            for src in range(2):
                for slot in range(CAP):
                    n = src * CAP + slot
                    live = (sel[src, b, CAP + slot].astype(F32) - 1.0) * 1e30
                    bias[i, xx, n * piece:(n + 1) * piece, :] = jnp.where(inside, live, -1e30)
        return 0

    tab_own.wait()
    tab_cross.wait()
    tab_other = pltpu.make_async_copy(tab, sel.at[1], tab_l.at[1])
    tab_other.start()
    tab_other.wait()
    lax.fori_loop(0, nz * 2, fill, 0)

    for k in range(min(nz + 1, chunks)):
        q_hop1(k)
    for k in range(min(nz - 1, chunks)):
        for d in range(1, nz - k):
            q_forward(k, d)

    def slot_body(j, _):
        k, second = j // 2, j % 2

        @pl.when((j >= 1) & (j <= pieces))
        def _():
            wy_cross(j - 1).start()

        @pl.when((k < chunks) & (second == 0))
        def _():
            for i in range(4):
                kv_own(k, i).wait()
                kv_cross(k, i).wait_recv()

            @pl.when(k + 2 < chunks)
            def _():
                kv_start(k + 2)

            @pl.when(k + nz + 1 < chunks)
            def _():
                q_hop1(k + nz + 1)

            for d in range(1, nz):
                @pl.when(k + nz - d < chunks)
                def _():
                    q_forward(k + nz - d, d)
            for h in range(hc):
                vt[h, :HDIM, :] = jnp.transpose(vb[k, :, :, h * HDIM:(h + 1) * HDIM].reshape(both, HDIM))
            hkw[...] = hkb[k].reshape(hkw.shape)
            hvw[...] = hvb[k].reshape(hvw.shape)

            def got(zs, _):
                q_to(zs, k, "c").wait_recv()
                return 0
            lax.fori_loop(0, nz, got, 0)

        @pl.when(k < chunks)
        def _():
            cc = jnp.where(second == 0, 1 - c, c)

            step = 2 if nz % 2 == 0 else 1

            def target(i, _):
                jobs = [(i * step + u, h) for u in range(step) for h in range(hc)]
                parts = [partial(k, t, cc, h) for t, h in jobs]

                @pl.when(second == 0)
                def _():
                    for (t, h), part in zip(jobs, parts):
                        put(ocs, mls, t, k, h, part)
                    for u in range(step):
                        for cpy in o_core(i * step + u, k):
                            cpy.start()

                @pl.when(second == 1)
                def _():
                    for u in range(step):
                        for cpy in o_core(i * step + u, k):
                            cpy.wait_recv()
                    for (t, h), part in zip(jobs, parts):
                        put(r, rml, t, k, h, merge(part, get(ocr, mlr, t, k, h)))
                return 0
            lax.fori_loop(0, nz // step, target, 0)

        def waves(i, _):
            wave = nz - 1 - i
            age = j - 1 - 2 * wave
            kk = age // 2

            @pl.when((age >= 0) & (age % 2 == 0) & (kk < chunks))
            def _():
                rs_step(kk, wave)

                @pl.when(wave == nz - 1)
                def _():
                    final(kk)
            return 0
        lax.fori_loop(0, nz, waves, 0)
        ready = j - 2 * nz

        @pl.when((ready >= 0) & (ready % 2 == 0))
        def _():
            project(ready // 2)
        return 0

    lax.fori_loop(0, 2 * chunks + 2 * nz - 1, slot_body, 0)

    def finish(i, _):
        y_cross(i).wait_recv()
        lanes = pl.ds(pl.multiple_of((hd * tiles + i) * tile, tile), tile)
        out[:, pl.ds(pl.multiple_of(i * tile, tile), tile)] = (acc[:, lanes] + yrecv[i].astype(F32)).astype(BF16)
        y_cross(i).wait_send()
        return 0

    lax.fori_loop(0, tiles, finish, 0)
    for g in range(late):
        atty_cross(g).wait_send()
    for n in range(pieces):
        wy_cross(n).wait_send()

    def drain(k, _):
        q_cross(k).wait_send()
        for i in range(4):
            kv_cross(k, i).wait_send()
        final_cross(k).wait_send()

        def each(t, _):
            q_to(t, k, "c").wait_send()
            for cpy in o_core(t, k):
                cpy.wait_send()

            @pl.when(has_right & (t <= z))
            def _():
                q_to(t, k, "r").wait_send()

            @pl.when(has_left & (t >= z))
            def _():
                q_to(t, k, "l").wait_send()

            @pl.when(t > z)
            def _():
                for cpy in o_right(t, k):
                    cpy.wait_send()

            @pl.when(t < z)
            def _():
                for cpy in o_left(t, k):
                    cpy.wait_send()
            return 0
        lax.fori_loop(0, nz, each, 0)
        return 0

    lax.fori_loop(0, chunks, drain, 0)


def reader_table(piece_readers, readers):
    hits = jnp.any(piece_readers[:, :, None] == jnp.arange(readers, dtype=jnp.int32)[None, None, :], axis=1)
    hits = hits.astype(jnp.int32)
    rank = jnp.cumsum(hits, axis=0) - hits
    index = jnp.arange(piece_readers.shape[0], dtype=jnp.int32)[:, None]
    where = [jnp.sum(jnp.where((hits > 0) & (rank == n), index, 0), axis=0) for n in range(CAP)]
    count = jnp.sum(hits, axis=0)
    return jnp.stack(where + [(count > n).astype(jnp.int32) for n in range(CAP)], axis=1)


def local_fused(queries, cur_keys, cur_values, hist_keys, hist_values, piece_readers, out_weight):
    tok, width = queries.shape
    hist = hist_keys.shape[0]
    readers = lax.axis_size("seq")
    nz = readers // PLANE
    half_heads = width // HDIM // 2
    hc = 1
    out_width = out_weight.shape[1]
    tile = 512 if out_width % 1024 == 0 else HDIM
    tiles = out_width // 2 // tile
    late = 1
    chunks = half_heads // hc
    w = hc * HDIM
    both = 2 * tok
    piece = hist // piece_readers.shape[0]
    table = reader_table(piece_readers, readers)
    table = jnp.pad(table, ((0, 0), (0, HDIM - table.shape[1])))
    vm = pltpu.VMEM
    sem = pltpu.SemaphoreType.DMA
    o_buf = vm((nz, chunks, w, both), BF16)
    ml_buf = vm((nz, chunks, hc * 8, both), F32)
    scratch = [
        vm((nz * 2, chunks, 2, tok, w), BF16),
        vm((chunks, 2, tok, w), BF16), vm((chunks, 2, tok, w), BF16),
        vm((chunks, 2, hist, w), BF16), vm((chunks, 2, hist, w), BF16),
        vm((2, hist // piece, piece, w), BF16), vm((2, hist // piece, piece, w), BF16),
        o_buf, ml_buf, o_buf, ml_buf, o_buf, ml_buf, o_buf, ml_buf, o_buf, ml_buf,
        vm((chunks, tok, w), BF16), vm((2, chunks, tok, w), BF16),
        vm((nz * 2, 2, 2 * CAP * piece, both // 2 // HDIM * HDIM + HDIM), F32),
        vm((hc, HDIM + 16, both), BF16),
        vm((2, 2, w, out_width), BF16), vm((tok, out_width), F32),
        vm((tiles, tok, tile), BF16), vm((tiles, tok, tile), BF16),
        vm((late, 2, w, out_width // 2), BF16), vm((late, 2, tok, w), BF16),
    ]
    scratch += [sem((chunks,))] * 3 + [sem((4, chunks))] * 3 + [sem((nz, chunks))] * 18
    scratch += [sem((2, chunks))] + [sem((chunks,))] * 2 + [sem((tiles,))] * 2
    scratch += [sem((late * 8,))] * 2 + [sem((late,))] * 2
    scratch += [pltpu.SMEM((2, readers, HDIM), jnp.int32), vm((readers, HDIM), jnp.int32), sem((2,)), sem((1,)), sem((1,))]
    any_spec = pl.BlockSpec(memory_space=pl.ANY)
    flops = 4 * readers * tok * (2 * tok + 4 * CAP * piece) * width // 2
    return pl.pallas_call(
        functools.partial(kernel, nz, chunks, hc, piece),
        out_shape=jax.ShapeDtypeStruct((tok, out_width // 2), BF16),
        in_specs=[any_spec] * 7,
        out_specs=pl.BlockSpec(memory_space=pltpu.VMEM),
        scratch_shapes=scratch,
        compiler_params=pltpu.CompilerParams(
            collective_id=0, has_side_effects=True, vmem_limit_bytes=62 * 1024 * 1024),
        cost_estimate=pl.CostEstimate(flops=flops, bytes_accessed=12 * tok * width, transcendentals=flops // 512),
    )(table, queries, cur_keys, cur_values, hist_keys, hist_values, out_weight)


def passed_along(value, axis, by):
    length = lax.axis_size(axis)
    return lax.ppermute(value, axis, [(i, (i + by) % length) for i in range(length)])


def attend(totals, query_heads, key_val, valid_keys):
    run_max, run_num, run_sum = totals
    head_count = query_heads.shape[1]
    key_heads = key_val[0].reshape(-1, head_count, HDIM)
    val_heads = key_val[1].reshape(-1, head_count, HDIM)
    scores = jnp.einsum("qhd,khd->hqk", query_heads, key_heads, preferred_element_type=jnp.float32)
    scores = scores * (1.0 / math.sqrt(HDIM))
    if valid_keys is not None:
        scores = jnp.where(valid_keys[None, None, :], scores, -1e30)
    new_max = jnp.maximum(run_max, jnp.max(scores, axis=-1))
    weights = jnp.exp(scores - new_max[..., None])
    if valid_keys is not None:
        weights = jnp.where(valid_keys[None, None, :], weights, 0.0)
    fade_by = jnp.exp(run_max - new_max)
    product = jnp.einsum(
        "hqk,khd->hqd", weights.astype(jnp.bfloat16), val_heads, preferred_element_type=jnp.float32
    )
    run_num = run_num * fade_by[..., None] + product
    run_sum = run_sum * fade_by + jnp.sum(weights, axis=-1)
    return (new_max, run_num, run_sum)


def local(queries, cur_keys, cur_values, hist_keys, hist_values, piece_readers, out_weight):
    tok_rows = queries.shape[0]
    width = queries.shape[1]
    head_count = width // HDIM
    query_heads = queries.reshape(tok_rows, head_count, HDIM)
    reader_count = lax.axis_size("seq")
    owner_rows = piece_readers.shape[0]
    piece_len = hist_keys.shape[0] // owner_rows
    reader_ids = jnp.arange(reader_count, dtype=jnp.int32)
    hits = jnp.sum(
        (piece_readers[:, :, None] == reader_ids[None, None, :]).astype(jnp.int32), axis=1
    )
    earlier = jnp.cumsum(hits, axis=0) - hits
    slot_ids = jnp.arange(CAP, dtype=jnp.int32)
    select = hits[None, :, :] * (earlier[None, :, :] == slot_ids[:, None, None]).astype(jnp.int32)
    select = jnp.transpose(select, (2, 0, 1))
    slot_full = jnp.sum(select, axis=2)[None, :, :]
    stacked = jnp.stack([hist_keys, hist_values]).reshape(2, owner_rows, piece_len * width)
    outgoing = jnp.einsum(
        "rcp,spx->srcx", select.astype(jnp.bfloat16), stacked, preferred_element_type=jnp.float32
    ).astype(jnp.bfloat16)
    arrived, arrived_full = (
        lax.all_to_all(outgoing, "seq", split_axis=1, concat_axis=1, tiled=True),
        lax.all_to_all(slot_full, "seq", split_axis=1, concat_axis=1, tiled=True),
    )
    hist_kv = arrived.reshape(2, -1, width)
    valid_keys = jnp.repeat(arrived_full.reshape(-1), piece_len) > 0
    start_totals = (
        jnp.full((head_count, tok_rows), -1e30, jnp.float32),
        jnp.zeros((head_count, tok_rows, HDIM), jnp.float32),
        jnp.zeros((head_count, tok_rows), jnp.float32),
    )
    totals = attend(start_totals, query_heads, hist_kv, valid_keys)
    own_block = jnp.stack([cur_keys, cur_values])
    totals = attend(totals, query_heads, own_block, None)

    def cycle_turn(step_idx, loop_state):
        travel, inner = loop_state
        travel = passed_along(travel, "seq", 1)
        return (travel, attend(inner, query_heads, travel, None))

    travel_end, totals = lax.fori_loop(0, reader_count - 1, cycle_turn, (own_block, totals))
    run_max, run_num, run_sum = totals
    attended = run_num / run_sum[..., None]
    attended = jnp.transpose(attended, (1, 0, 2)).reshape(tok_rows, width).astype(jnp.bfloat16)
    partial_out = jnp.dot(attended, out_weight, preferred_element_type=jnp.float32)
    return lax.psum_scatter(
        partial_out.astype(jnp.bfloat16), "head", scatter_dimension=1, tiled=True
    )


def solution(mesh):
    placed = (
        P("seq", "head"),
        P("seq", "head"),
        P("seq", "head"),
        P("seq", "head"),
        P("seq", "head"),
        P("seq", None),
        P("head", None),
    )

    def run(*args):
        heads = args[0].shape[1] // mesh.shape["head"] // HDIM
        whole_planes = mesh.shape["seq"] % PLANE == 0 and heads % 2 == 0 and heads > 4 and mesh.shape["head"] == 2
        whole_planes = whole_planes and args[0].shape[0] // mesh.shape["seq"] % HDIM == HDIM // 2
        return jax.shard_map(
            local_fused if whole_planes else local,
            mesh=mesh, in_specs=placed, out_specs=P("seq", "head"), check_vma=False,
        )(*args)

    return run
```
